32 devices in a mesh: dp: 4 (over z), row: 4 (over y, core), col: 2 (over x).
Axes of the slice: x: 2, y: 2, z: 4, core: 2. Of those that a mesh axis runs over, the one named last changes fastest.
Arguments:
- tokens: bfloat16 [16384, 1024], P(('dp', 'row'), 'col'), may hold values from -6 to 6
- seq_lengths: int32 [4, 2], P('dp'), may hold values from 1024 to 3072, as said below
- attn_gain: float32 [1024], P('col'), may hold values from 0.5 to 1.5
- q_weight: bfloat16 [1024, 1024], P('col', 'row'), may hold values from -0.1875 to 0.1875
- k_weight: bfloat16 [1024, 512], P('col', 'row'), may hold values from -0.1875 to 0.1875
- v_weight: bfloat16 [1024, 512], P('col', 'row'), may hold values from -0.1875 to 0.1875
- q_gain: float32 [64], replicated, may hold values from 0.5 to 1.5
- k_gain: float32 [64], replicated, may hold values from 0.5 to 1.5
- o_weight: bfloat16 [1024, 1024], P('row', 'col'), may hold values from -0.75 to 0.75
- ffn_gain: float32 [1024], P('col'), may hold values from 0.5 to 1.5
- gate_weight: bfloat16 [1024, 4608], P('col', 'row'), may hold values from -0.1875 to 0.1875
- up_weight: bfloat16 [1024, 4608], P('col', 'row'), may hold values from -0.1875 to 0.1875
- down_weight: bfloat16 [4608, 1024], P('row', 'col'), may hold values from -0.09375 to 0.09375
- cotangent: bfloat16 [16384, 1024], P(('dp', 'row'), 'col'), may hold values from -6 to 6
Outputs:
- output: bfloat16 [16384, 1024], P(('dp', 'row'), 'col')
- input_grad: float32 [16384, 1024], P(('dp', 'row'), 'col')
- attn_gain_grad: float32 [1024], P('col')
- q_weight_grad: float32 [1024, 1024], P('col', 'row')
- k_weight_grad: float32 [1024, 512], P('col', 'row')
- v_weight_grad: float32 [1024, 512], P('col', 'row')
- q_gain_grad: float32 [64], replicated
- k_gain_grad: float32 [64], replicated
- o_weight_grad: float32 [1024, 1024], P('row', 'col')
- ffn_gain_grad: float32 [1024], P('col')
- gate_weight_grad: float32 [1024, 4608], P('col', 'row')
- up_weight_grad: float32 [1024, 4608], P('col', 'row')
- down_weight_grad: float32 [4608, 1024], P('row', 'col')
The draws below stay inside these ranges and needn't reach their ends.
Inputs may be any that keep to these rules, and one draw needn't show every extreme that they name: `seq_lengths`: in each group the first sequence is shorter than 2048 and the two lengths sum to 4096; in every draw some group has lengths 1024 and 3072.
All inputs are finite; a program needn't handle non-finite values.
Results may differ from the reference program's by a relative error of at most 0.014.
Values may be sent and summed in bfloat16 or wider, within the bound.
No kernel may reach another device: no remote copies, remote signals or barrier semaphores. Data moves between devices by JAX's collectives and lax.ppermute only.
A program may use at most 256 MiB of HBM per device.

```python
import jax
import jax.numpy as jnp
from jax import lax

D = 1024
H = 16
KV = 8
HD = 64
FF = 4608
GRP = 4096
MIN_LEN = 1024
TOKENS = 16384
N_DP = 4


def draw_seq_lengths(key, part):
    key = jax.random.fold_in(key, 17)
    short_key, pick_key = jax.random.split(key)
    shorter = jax.random.randint(short_key, (N_DP,), MIN_LEN, GRP // 2)
    chosen = jax.random.randint(pick_key, (), 0, N_DP)
    shorter = jnp.where(jnp.arange(N_DP) == chosen, MIN_LEN, shorter)
    return jnp.stack([shorter, GRP - shorter], axis=1).astype(jnp.int32)


def shard_levels(key, dims, shards, low, top_value):
    loudness = 1.0
    for dim, parts in shards:
        heights = jax.random.uniform(jax.random.fold_in(jax.random.fold_in(key, 6), dim), (parts,), jnp.float32, low / len(shards), top_value / len(shards))
        loudness = loudness * jnp.repeat(jnp.exp(heights), dims[dim] // parts).reshape((-1,) + (1,) * (len(dims) - 1 - dim))
    return loudness


def scatter_about(rng, shape, scale, most, shards=(), kind=jnp.bfloat16):
    gain = shard_levels(rng, shape, shards, -0.22, 0.18) if shards else 1.0
    values = jax.random.normal(rng, shape, jnp.float32) * scale * gain
    return jnp.minimum(jnp.maximum(values, -most), most).astype(kind)


def setup_inputs(seed: int = 0) -> dict:
    streams_of = jax.random.split(jax.random.key(seed), 15)
    return {
        "tokens": scatter_about(streams_of[0], (TOKENS, D), 1.0, 6.0, ((0, 16), (1, 2))),
        "seq_lengths": draw_seq_lengths(jax.random.fold_in(streams_of[14], 71), 0),
        "attn_gain": jnp.clip(1.0 + 0.1 * jax.random.normal(streams_of[2], (D,), jnp.float32), 0.5, 1.5),
        "q_weight": scatter_about(streams_of[3], (D, H * HD), D ** -0.5, 0.1875, ((0, 2), (1, 4))),
        "k_weight": scatter_about(streams_of[4], (D, KV * HD), D ** -0.5, 0.1875, ((0, 2), (1, 4))),
        "v_weight": scatter_about(streams_of[5], (D, KV * HD), D ** -0.5, 0.1875, ((0, 2), (1, 4))),
        "q_gain": jnp.clip(1.0 + 0.1 * jax.random.normal(streams_of[6], (HD,), jnp.float32), 0.5, 1.5),
        "k_gain": jnp.clip(1.0 + 0.1 * jax.random.normal(streams_of[7], (HD,), jnp.float32), 0.5, 1.5),
        "o_weight": scatter_about(streams_of[8], (H * HD, D), (H * HD // 16) ** -0.5, 0.75, ((0, 4), (1, 2))),
        "ffn_gain": jnp.clip(1.0 + 0.1 * jax.random.normal(streams_of[9], (D,), jnp.float32), 0.5, 1.5),
        "gate_weight": scatter_about(streams_of[10], (D, FF), D ** -0.5, 0.1875, ((0, 2), (1, 4))),
        "up_weight": scatter_about(streams_of[11], (D, FF), D ** -0.5, 0.1875, ((0, 2), (1, 4))),
        "down_weight": scatter_about(streams_of[12], (FF, D), FF ** -0.5, 0.09375, ((0, 4), (1, 2))),
        "cotangent": scatter_about(streams_of[13], (TOKENS, D), 1.0, 6.0, ((0, 16), (1, 2))),
    }


EPSILON = 1e-05
ROPE_BASE = 1000000.0
MASKED_SCORE = -1e+30
HIGHEST = lax.Precision.HIGHEST

@jax.custom_vjp
def low(v):
    return lax.optimization_barrier(v.astype(jnp.bfloat16)).astype(jnp.float32)

@jax.custom_vjp
def low_back(v):
    return v

def low_keep(v):
    return (low(v), None)

def low_pass(kept, grad):
    return (grad,)

def back_keep(v):
    return (v, None)

def back_low(kept, grad):
    return (low(grad),)
low.defvjp(low_keep, low_pass)
low_back.defvjp(back_keep, back_low)

def segment_info(lengths, total_rows):
    seq_ends = jnp.cumsum(lengths).astype(jnp.int32)
    token_index = jnp.arange(total_rows, dtype=jnp.int32)
    seq_numbers = jnp.arange(lengths.shape[0], dtype=jnp.int32)
    sequence_ids = lax.optimization_barrier(jnp.sum((token_index[:, None] >= seq_ends[None, :]).astype(jnp.int32), axis=1)).astype(jnp.int32)
    starts = (seq_ends - lengths).astype(jnp.int32)
    seq_first = lax.optimization_barrier(jnp.sum(jnp.where(sequence_ids[:, None] == seq_numbers[None, :], starts[None, :], 0), axis=1)).astype(jnp.int32)
    return (token_index, sequence_ids, token_index - seq_first)

def rope_tables(positions, head_width):
    half_width = head_width // 2
    frequencies = ROPE_BASE ** (-(jnp.arange(half_width, dtype=jnp.float32) * 2.0) / head_width)
    angles = positions.astype(jnp.float32)[:, None] * frequencies[None, :]
    cosine_table = jnp.cos(angles)
    sine_table = jnp.sin(angles)
    return (jnp.concatenate([cosine_table, cosine_table], axis=1), jnp.concatenate([sine_table, sine_table], axis=1))

def rotate(values, cosine_table, sine_table):
    half_width = values.shape[-1] // 2
    turned = jnp.concatenate([-values[..., half_width:], values[..., :half_width]], axis=-1)
    return values * cosine_table[:, None, :] + turned * sine_table[:, None, :]

def norm_rows(values, gain_vector):
    return values * lax.rsqrt(lax.optimization_barrier(jnp.mean(values * values, axis=-1, keepdims=True)) + EPSILON) * gain_vector

def block_forward(inputs, attn_gain, q_weight, k_weight, v_weight, q_gain, k_gain, o_weight, ffn_gain, gate_weight, up_weight, down_weight, token_index, sequence_ids, cosine_table, sine_table):
    total_rows = inputs.shape[0]
    query_cols = H * HD
    kv_cols = KV * HD
    normed_one = low(norm_rows(inputs, attn_gain))
    projected = low_back(jnp.dot(normed_one, jnp.concatenate([q_weight, k_weight, v_weight], axis=1), precision=HIGHEST))
    queries = low(rotate(norm_rows(projected[:, :query_cols].reshape(total_rows, H, HD), q_gain), cosine_table, sine_table))
    keys = low(rotate(norm_rows(projected[:, query_cols:query_cols + kv_cols].reshape(total_rows, KV, HD), k_gain), cosine_table, sine_table))
    values = low(projected[:, query_cols + kv_cols:].reshape(total_rows, KV, HD))
    block_rows = min(512, total_rows)
    block_count = total_rows // block_rows
    query_groups = queries.reshape(block_count, block_rows, KV, H // KV, HD)
    score_scale = HD ** (-0.5)

    def attend(block_id):
        query_block = query_groups[block_id]
        row_index = lax.dynamic_slice_in_dim(token_index, block_id * block_rows, block_rows)
        row_seq = lax.dynamic_slice_in_dim(sequence_ids, block_id * block_rows, block_rows)
        scores = jnp.einsum('qkgd,nkd->kgqn', query_block, keys, precision=HIGHEST) * score_scale
        scores = low_back(scores)
        allowed = (sequence_ids[None, :] == row_seq[:, None]) & (token_index[None, :] <= row_index[:, None])
        scores = jnp.where(allowed[None, None], scores, MASKED_SCORE)
        probabilities = low(jax.nn.softmax(scores, axis=-1))
        attended = jnp.einsum('kgqn,nkd->qkgd', probabilities, values, precision=HIGHEST)
        return attended.reshape(block_rows, query_cols)
    attended = lax.map(jax.checkpoint(attend), jnp.arange(block_count, dtype=jnp.int32)).reshape(total_rows, query_cols)
    attended = low_back(low(attended))
    residual = inputs + low_back(jnp.dot(attended, o_weight, precision=HIGHEST))
    normed_two = low(norm_rows(residual, ffn_gain))
    gate_up = low_back(jnp.dot(normed_two, jnp.concatenate([gate_weight, up_weight], axis=1), precision=HIGHEST))
    hidden = low(jax.nn.silu(gate_up[:, :FF]) * gate_up[:, FF:])
    return residual + low_back(jnp.dot(hidden, down_weight, precision=HIGHEST))

def reference(tokens, seq_lengths, attn_gain, q_weight, k_weight, v_weight, q_gain, k_gain, o_weight, ffn_gain, gate_weight, up_weight, down_weight, cotangent):
    params = tuple((item.astype(jnp.float32) for item in (attn_gain, q_weight, k_weight, v_weight, q_gain, k_gain, o_weight, ffn_gain, gate_weight, up_weight, down_weight)))

    def one_group(carried, group_item):
        group_inputs, group_cot, lengths = group_item
        token_index, sequence_ids, positions = segment_info(lengths, GRP)
        cosine_table, sine_table = rope_tables(positions, HD)

        def forward(inputs, *weights):
            return block_forward(inputs, *weights, token_index, sequence_ids, cosine_table, sine_table)
        result, pullback = jax.vjp(forward, group_inputs.astype(jnp.float32), *params)
        grads = pullback(group_cot.astype(jnp.float32))
        updated = tuple((first_term + second_term for first_term, second_term in zip(carried, grads[1:])))
        return (updated, (result.astype(jnp.bfloat16), grads[0]))
    zero_grads = tuple((jnp.zeros(item.shape, jnp.float32) for item in params))
    summed, (outputs_all, input_grads) = lax.scan(one_group, zero_grads, (tokens.reshape(N_DP, GRP, D), cotangent.reshape(N_DP, GRP, D), seq_lengths))
    return (outputs_all.reshape(TOKENS, D), input_grads.reshape(TOKENS, D), summed[0], summed[1], summed[2], summed[3], summed[4], summed[5], summed[6], summed[7], summed[8], summed[9], summed[10])
```

```python
import functools

import jax
import jax.numpy as jnp
from jax import lax
from jax.experimental import pallas as pl
from jax.experimental.pallas import tpu as pltpu
from jax.sharding import PartitionSpec as P

EPSILON = 1e-05
ROPE_BASE = 1000000.0
MASKED_SCORE = -1e30
F32 = jnp.float32
BF16 = jnp.bfloat16
LANES = 128
VMEM_LIMIT = 56 * 1024 * 1024


def swap(values, axis, distance):
    count = lax.axis_size(axis)
    return lax.ppermute(values, axis, [(i, i ^ distance) for i in range(count)])


def dot(a, b):
    return jnp.dot(a, b, preferred_element_type=F32)


def dot_nt(a, b):
    return lax.dot_general(a, b, (((1,), (1,)), ((), ())), preferred_element_type=F32)


def dot_tn(a, b):
    return lax.dot_general(a, b, (((0,), (0,)), ((), ())), preferred_element_type=F32)


def gather_row(values):
    core = swap(values, "row", 1)
    far = swap(values, "row", 2)
    return [values, core, far, swap(far, "row", 1)]


def scatter_row(parts):
    far = parts[2].astype(F32) + swap(parts[3], "row", 1).astype(F32)
    far = swap(far.astype(BF16), "row", 2)
    near = parts[0].astype(F32) + swap(parts[1], "row", 1).astype(F32)
    return near + far.astype(F32)


def exchange_row(parts):
    return [parts[0]] + [swap(parts[k], "row", k) for k in (1, 2, 3)]


def sub_block(idx, col):
    return jnp.where(col == 0, 3 * idx, 1 + idx)


def natural_block(i, row, col):
    return 4 * ((i >> 1) ^ row) + sub_block(i & 1, col)


def is_other(block, col):
    return ((((block & 3) + 1) >> 1) & 1) ^ col


def storage_block(block, row):
    return (((block >> 2) ^ row) << 1) + ((block & 3) >> 1)


def own_before(block, col):
    sub = block & 3
    first = (sub > 0).astype(jnp.int32)
    second = (sub > 1).astype(jnp.int32) + (sub > 2).astype(jnp.int32)
    return 2 * (block >> 2) + jnp.where(col == 0, first, second)


def lane_of(rows):
    return lax.broadcasted_iota(jnp.int32, (rows, LANES), 1)


def second_sequence(block, size, boundary):
    token = block * size + lax.broadcasted_iota(jnp.int32, (size, LANES), 0)
    return token >= boundary


def half_pick(chunk, which):
    return chunk if which == 0 else pltpu.roll(chunk, 64, 1)


def query_pieces(queries, block, size, boundary, pair):
    lane = lane_of(size)
    second = second_sequence(block, size, boundary)
    extra = jnp.where(lane == 64, jnp.where(second, 0.0, 1.0), jnp.where(second, 1.0, 0.0))
    extra = jnp.where(lane <= 65, extra, 0.0)
    chunk = queries[:, pair * LANES : (pair + 1) * LANES].astype(F32)
    return jnp.concatenate(
        [jnp.where(lane < 64, half_pick(chunk, w), extra).astype(BF16) for w in (0, 1)], axis=0
    )


def build_keys(kv, block, size, boundary, g):
    lane = lane_of(size)
    second = second_sequence(block, size, boundary)
    extra = jnp.where(
        lane == 64,
        jnp.where(second, MASKED_SCORE, 0.0),
        jnp.where(second, 0.0, MASKED_SCORE),
    )
    extra = jnp.where(lane <= 65, extra, 0.0)
    ones = jnp.where(lane <= 65, 1.0, 0.0)
    key = jnp.where(lane < 64, half_pick(kv[:, :LANES], g), extra)
    value = jnp.where(lane < 64, half_pick(kv[:, LANES:], g), ones)
    return key.astype(BF16), value.astype(BF16)


def attention_forward(
    place, q_ref, own_ref, other_ref, out_ref, inverse_ref, key_ref, value_ref, *, size, blocks
):
    row, col, boundary = place[0], place[1], place[2]

    def fill(i, carry):
        rows = pl.ds(pl.multiple_of(i * size, size), size)
        for part, ref in ((0, own_ref), (1, other_ref)):
            kv = ref[rows, :].astype(F32)
            block = natural_block(i, row, col ^ part)
            target = pl.ds(pl.multiple_of((part * blocks + i) * size, size), size)
            for g in range(2):
                key, value = build_keys(kv, block, size, boundary, g)
                key_ref[g, target, :] = key
                value_ref[g, target, :] = value
        return carry

    lax.fori_loop(0, blocks, fill, 0)
    later = lax.broadcasted_iota(jnp.int32, (2 * size, size), 0) % size
    allowed = lax.broadcasted_iota(jnp.int32, (2 * size, size), 1) <= later
    lane = lane_of(size)

    def one_block(i, carry):
        rows = pl.ds(pl.multiple_of(i * size, size), size)
        block = natural_block(i, row, col)
        queries = q_ref[rows, :]
        packed = [query_pieces(queries, block, size, boundary, g) for g in range(2)]

        def term(j, g, diagonal):
            start = (is_other(j, col) * blocks + storage_block(j, row)) * size
            keys = pl.ds(pl.multiple_of(start, size), size)
            weights = jnp.exp(dot_nt(packed[g], key_ref[g, keys, :]))
            if diagonal:
                weights = jnp.where(allowed, weights, 0.0)
            return dot(weights.astype(BF16), value_ref[g, keys, :])

        def step(j, sums):
            return tuple(sums[g] + term(j, g, False) for g in range(2))

        first = jnp.where(block * size >= boundary, boundary // size, 0)
        sums = tuple(term(block, g, True) for g in range(2))
        sums = lax.fori_loop(first, block, step, sums)
        for g in range(2):
            inverse = 1.0 / sums[g][:, 64:65]
            scaled = sums[g] * inverse
            columns = slice(g * LANES, (g + 1) * LANES)
            joined = jnp.where(lane < 64, scaled[:size], pltpu.roll(scaled[size:], 64, 1))
            out_ref[rows, columns] = joined.astype(BF16)
            inverse_ref[rows, columns] = jnp.where(lane < 64, inverse[:size], inverse[size:])
        return carry

    lax.fori_loop(0, blocks, one_block, 0)


def attention_backward(
    place,
    q_ref,
    own_ref,
    other_ref,
    out_ref,
    inverse_ref,
    grad_ref,
    dq_ref,
    dkv_own_ref,
    dkv_other_ref,
    key_ref,
    value_ref,
    turned_ref,
    packed_ref,
    packed_grad_ref,
    dq_sum,
    dk_sum,
    dv_sum,
    *,
    size,
    blocks,
):
    row, col, boundary = place[0], place[1], place[2]
    lane = lane_of(size)

    def fill(i, carry):
        rows = pl.ds(pl.multiple_of(i * size, size), size)
        for part, ref in ((0, own_ref), (1, other_ref)):
            kv = ref[rows, :].astype(F32)
            block = natural_block(i, row, col ^ part)
            target = pl.ds(pl.multiple_of((part * blocks + i) * size, size), size)
            for g in range(2):
                key, value = build_keys(kv, block, size, boundary, g)
                key_ref[g, target, :] = key
                value_ref[g, target, :] = value
            turned_ref[:, target] = kv[:, :LANES].T.astype(BF16)
        block = natural_block(i, row, col)
        wide = pl.ds(pl.multiple_of(i * 2 * size, 2 * size), 2 * size)
        queries = q_ref[rows, :]
        for g in range(2):
            columns = slice(g * LANES, (g + 1) * LANES)
            packed_ref[g, wide, :] = query_pieces(queries, block, size, boundary, g)
            scaled = grad_ref[rows, columns].astype(F32) * inverse_ref[rows, columns]
            product = scaled * out_ref[rows, columns].astype(F32)
            pieces = []
            for w in (0, 1):
                total = -jnp.sum(
                    jnp.where((lane >= 64) if w else (lane < 64), product, 0.0), axis=1, keepdims=True
                )
                high = total.astype(BF16).astype(F32)
                extra = jnp.where(lane == 64, high, jnp.where(lane == 65, total - high, 0.0))
                pieces.append(jnp.where(lane < 64, half_pick(scaled, w), extra).astype(BF16))
            packed_grad_ref[g, wide, :] = jnp.concatenate(pieces, axis=0)
            dq_sum[g, :, wide] = jnp.zeros((64, 2 * size), F32)
        return carry

    lax.fori_loop(0, blocks, fill, 0)
    later = lax.broadcasted_iota(jnp.int32, (size, 2 * size), 1) % size
    allowed = lax.broadcasted_iota(jnp.int32, (size, 2 * size), 0) <= later

    def pair(start, i, diagonal):
        keys = pl.ds(start, size)
        wide = pl.ds(pl.multiple_of(i * 2 * size, 2 * size), 2 * size)
        for g in range(2):
            queries = packed_ref[g, wide, :]
            grads = packed_grad_ref[g, wide, :]
            weights = jnp.exp(dot_nt(key_ref[g, keys, :], queries))
            if diagonal:
                weights = jnp.where(allowed, weights, 0.0)
            change = dot_nt(value_ref[g, keys, :], grads)
            score = (weights * change).astype(BF16)
            dv_sum[g] += dot(weights.astype(BF16), grads)
            dk_sum[g] += dot(score, queries)
            dq_sum[g, :, wide] += dot(turned_ref[64 * g : 64 * (g + 1), keys], score)

    def one_block(j, carry):
        other = is_other(j, col)
        place_in = storage_block(j, row)
        start = pl.multiple_of((other * blocks + place_in) * size, size)
        dk_sum[...] = jnp.zeros_like(dk_sum)
        dv_sum[...] = jnp.zeros_like(dv_sum)
        last = jnp.where((j + 1) * size <= boundary, (boundary - 1) // size, 2 * blocks - 1)
        begin = own_before(j, col) + 1 - other
        end = own_before(last + 1, col)

        @pl.when(other == 0)
        def _():
            pair(start, place_in, True)

        def step(n, carry):
            pair(start, (((n >> 1) ^ row) << 1) + (n & 1), False)
            return carry

        lax.fori_loop(begin, end, step, 0)
        key_grad = jnp.where(lane < 64, dk_sum[0], pltpu.roll(dk_sum[1], 64, 1))
        value_grad = jnp.where(lane < 64, dv_sum[0], pltpu.roll(dv_sum[1], 64, 1))
        rows = pl.ds(pl.multiple_of(place_in * size, size), size)

        @pl.when(other == 0)
        def _():
            dkv_own_ref[rows, :LANES] = key_grad
            dkv_own_ref[rows, LANES:] = value_grad

        @pl.when(other == 1)
        def _():
            dkv_other_ref[rows, :LANES] = key_grad.astype(BF16)
            dkv_other_ref[rows, LANES:] = value_grad.astype(BF16)

        return carry

    lax.fori_loop(0, 2 * blocks, one_block, 0)

    def finish(i, carry):
        rows = pl.ds(pl.multiple_of(i * size, size), size)
        for g in range(2):
            wide = pl.multiple_of(i * 2 * size, 2 * size)
            stacked = jnp.concatenate(
                [dq_sum[g, :, pl.ds(wide, size)], dq_sum[g, :, pl.ds(wide + size, size)]], axis=0
            )
            dq_ref[rows, g * LANES : (g + 1) * LANES] = stacked.T
        return carry

    lax.fori_loop(0, blocks, finish, 0)


def head_totals(values):
    a = lax.broadcasted_iota(jnp.int32, (LANES, LANES), 0) // 64
    b = lax.broadcasted_iota(jnp.int32, (LANES, LANES), 1) // 64
    same = jnp.where(a == b, 1.0, 0.0).astype(BF16)
    high = values.astype(BF16)
    low = (values - high.astype(F32)).astype(BF16)
    return dot(high, same) + dot(low, same)


def turned_lanes(values):
    first = lane_of(values.shape[0]) % 64 < 32
    return jnp.where(first, pltpu.roll(values, LANES - 32, 1), pltpu.roll(values, 32, 1))


def prepare_kernel(pre_ref, cos_ref, sin_ref, gain_ref, q_ref, kv_ref, *, scale):
    for n in range(3):
        values = pre_ref[:, n * LANES : (n + 1) * LANES]
        inverse = lax.rsqrt(head_totals(values * values) / 64 + EPSILON)
        normed = values * inverse * gain_ref[(0 if n < 2 else 1) : (1 if n < 2 else 2), :]
        rotated = normed * cos_ref[...] + turned_lanes(normed) * sin_ref[...]
        if n < 2:
            q_ref[:, n * LANES : (n + 1) * LANES] = (
                rotated.astype(BF16).astype(F32) * scale
            ).astype(BF16)
        else:
            kv_ref[:, :LANES] = rotated.astype(BF16)
    kv_ref[:, LANES:] = pre_ref[:, 3 * LANES :].astype(BF16)


def prepare_back_kernel(
    pre_ref, cos_ref, sin_ref, gain_ref, dq_ref, own_ref, got_ref, out_ref, sums_ref, *, scale
):
    @pl.when(pl.program_id(0) == 0)
    def _():
        sums_ref[...] = jnp.zeros_like(sums_ref)

    for n in range(3):
        columns = slice(n * LANES, (n + 1) * LANES)
        values = pre_ref[:, columns]
        inverse = lax.rsqrt(head_totals(values * values) / 64 + EPSILON)
        if n < 2:
            grad = dq_ref[:, columns] * scale
        else:
            grad = own_ref[:, :LANES] + got_ref[:, :LANES].astype(F32)
        grad = grad * cos_ref[...] - turned_lanes(grad) * sin_ref[...]
        hat = values * inverse
        sums_ref[0:1, columns] += jnp.sum(grad * hat, axis=0, keepdims=True)
        scaled = grad * gain_ref[(0 if n < 2 else 1) : (1 if n < 2 else 2), :]
        mean = head_totals(scaled * hat) / 64
        out_ref[:, columns] = (inverse * (scaled - hat * mean)).astype(BF16)
    out_ref[:, 3 * LANES :] = (own_ref[:, LANES:] + got_ref[:, LANES:].astype(F32)).astype(BF16)


def norm_rows(values, gain):
    inverse = lax.rsqrt(jnp.mean(values * values, axis=1, keepdims=True) + EPSILON)
    return (values * inverse * gain).astype(BF16), inverse


def norm_backward(values, inverse, gain, grad):
    gain_grad = jnp.sum(grad * values * inverse, axis=0)
    scaled = grad * gain
    inner = jnp.mean(scaled * values, axis=1, keepdims=True)
    return scaled * inverse - values * (inverse * inverse * inverse * inner), gain_grad


def body(
    tokens,
    seq_lengths,
    attn_gain,
    q_weight,
    k_weight,
    v_weight,
    q_gain,
    k_gain,
    o_weight,
    ffn_gain,
    gate_weight,
    up_weight,
    down_weight,
    cotangent,
):
    row, col = lax.axis_index("row"), lax.axis_index("col")
    local_rows, width = tokens.shape
    size = local_rows // 4
    own_rows = 2 * size
    blocks = 8
    all_rows = blocks * size
    head = q_gain.shape[0]
    scale = head ** (-0.5)
    hidden_cols = gate_weight.shape[1]
    boundary = seq_lengths[0, 0]

    def mine(x):
        outer = jnp.concatenate([x[:size], x[3 * size :]], axis=0)
        inner = x[size : 3 * size]
        return jnp.where(col == 0, outer, inner), jnp.where(col == 0, inner, outer)

    def to_whole(x):
        keep, give = mine(x)
        return jnp.concatenate([keep, swap(give, "col", 1)], axis=1)

    def from_whole(keep, got):
        outer = jnp.where(col == 0, keep, got)
        inner = jnp.where(col == 0, got, keep)
        return jnp.concatenate([outer[:size], inner, outer[size:]], axis=0)

    def both(x, axis):
        return jnp.concatenate([x, swap(x, "col", 1)], axis=axis)

    tokens_own = to_whole(tokens)
    w_qkv = both(jnp.concatenate([q_weight, k_weight, v_weight], axis=1), 0)
    gains = both(jnp.stack([attn_gain, ffn_gain]), 1)
    gain_one, gain_two = gains[0], gains[1]
    cot_own = to_whole(cotangent)
    w_o = jnp.concatenate(gather_row(both(o_weight, 1)), axis=0)

    index = jnp.arange(all_rows, dtype=jnp.int32)
    token = natural_block(index // size, row, col) * size + index % size
    position = jnp.where(token >= boundary, token - boundary, token)
    lane = jnp.arange(LANES, dtype=jnp.int32)
    frequency = ROPE_BASE ** (-((jnp.arange(head // 2, dtype=F32)) * 2.0) / head)
    angle = position.astype(F32)[:, None] * frequency[None, :]
    cos_table = jnp.tile(jnp.cos(angle), (1, LANES // (head // 2)))
    sin_table = jnp.tile(jnp.sin(angle), (1, LANES // (head // 2)))
    sin_table = jnp.where((lane % head < head // 2)[None, :], -sin_table, sin_table)
    head_gains = jnp.stack([jnp.tile(q_gain, 2), jnp.tile(k_gain, 2)])

    inputs = tokens_own.astype(F32)
    normed_one, inverse_one = norm_rows(inputs, gain_one)
    normed_one_all = jnp.concatenate(gather_row(normed_one), axis=0)
    projected = dot(normed_one_all, w_qkv)

    def tile(columns):
        return pl.BlockSpec((size, columns), lambda i: (i, 0))

    gain_spec = pl.BlockSpec((2, LANES), lambda i: (0, 0))
    queries, kv_own = pl.pallas_call(
        functools.partial(prepare_kernel, scale=scale),
        grid=(blocks,),
        in_specs=[tile(512), tile(LANES), tile(LANES), gain_spec],
        out_specs=[tile(256), tile(256)],
        out_shape=[jax.ShapeDtypeStruct((all_rows, 256), BF16)] * 2,
        name="prepare",
    )(projected, cos_table, sin_table, head_gains)
    kv_other = swap(kv_own, "col", 1)

    place = jnp.stack([row.astype(jnp.int32), col.astype(jnp.int32), boundary.astype(jnp.int32)])
    whole = pl.BlockSpec(memory_space=pltpu.VMEM)
    smem = pl.BlockSpec(memory_space=pltpu.SMEM)
    attended, inverse_total = pl.pallas_call(
        functools.partial(attention_forward, size=size, blocks=blocks),
        in_specs=[smem] + [whole] * 3,
        out_specs=[whole] * 2,
        out_shape=[
            jax.ShapeDtypeStruct((all_rows, 256), BF16),
            jax.ShapeDtypeStruct((all_rows, 256), F32),
        ],
        scratch_shapes=[pltpu.VMEM((2, 2 * all_rows, LANES), BF16)] * 2,
        compiler_params=pltpu.CompilerParams(vmem_limit_bytes=VMEM_LIMIT),
        name="attend",
    )(place, queries, kv_own, kv_other)

    def chunks(x):
        return [x[k * own_rows : (k + 1) * own_rows] for k in range(4)]

    attended_own = jnp.concatenate(exchange_row(chunks(attended)), axis=1)
    residual = inputs + dot(attended_own, w_o)
    normed_two, inverse_two = norm_rows(residual, gain_two)
    w_gate, w_up = both(gate_weight, 0), both(up_weight, 0)
    w_down = both(down_weight, 1)
    normed_two_all = jnp.concatenate(gather_row(normed_two), axis=0)
    gate = dot(normed_two_all, w_gate)
    up = dot(normed_two_all, w_up)
    sigmoid = 1.0 / (1.0 + jnp.exp(-gate))
    hidden = (gate * sigmoid * up).astype(BF16)
    cot_all = jnp.concatenate(gather_row(cot_own), axis=0)
    hidden_grad = dot_nt(cot_all, w_down)
    gate_grad = (hidden_grad * up * (sigmoid * (1.0 + gate * (1.0 - sigmoid)))).astype(BF16)
    up_grad = (hidden_grad * gate * sigmoid).astype(BF16)
    normed_two_grad = scatter_row(
        chunks((dot_nt(gate_grad, w_gate) + dot_nt(up_grad, w_up)).astype(BF16))
    )
    residual_part, ffn_gain_grad = norm_backward(residual, inverse_two, gain_two, normed_two_grad)
    residual_grad = cot_own.astype(F32) + residual_part
    branch_grad = residual_grad.astype(BF16)
    attended_grad = dot_nt(branch_grad, w_o).astype(BF16)
    attended_grad = jnp.concatenate(
        exchange_row([attended_grad[:, k * 256 : (k + 1) * 256] for k in range(4)]), axis=0
    )

    def fold_rows(x):
        got = swap(x[width:].astype(BF16), "col", 1)
        return (x[:width] + got.astype(F32)).astype(BF16)

    def fold_cols(x):
        got = swap(x[:, width:].astype(BF16), "col", 1)
        return (x[:, :width] + got.astype(F32)).astype(BF16)

    down_grad = fold_cols(dot_tn(hidden, cot_all))
    gate_weight_grad = fold_rows(dot_tn(normed_two_all, gate_grad))
    up_weight_grad = fold_rows(dot_tn(normed_two_all, up_grad))
    down_grad = lax.psum(down_grad, "dp")
    gate_weight_grad, down_grad = lax.optimization_barrier((gate_weight_grad, down_grad))
    gate_weight_grad = lax.psum(gate_weight_grad, "dp")
    up_weight_grad, gate_weight_grad = lax.optimization_barrier((up_weight_grad, gate_weight_grad))
    up_weight_grad = lax.psum(up_weight_grad, "dp")

    ffn_out = scatter_row(chunks(dot(hidden, w_down).astype(BF16)))
    output = (residual + ffn_out).astype(BF16)
    output = from_whole(output[:, :width], swap(output[:, width:], "col", 1))

    o_part = dot_tn(attended_own, branch_grad)
    o_part = fold_cols(o_part)
    o_rows = o_weight.shape[0]
    o_grad = scatter_row([o_part[k * o_rows : (k + 1) * o_rows] for k in range(4)]).astype(BF16)

    dq, dkv_own, dkv_other = pl.pallas_call(
        functools.partial(attention_backward, size=size, blocks=blocks),
        in_specs=[smem] + [whole] * 6,
        out_specs=[whole] * 3,
        out_shape=[
            jax.ShapeDtypeStruct((all_rows, 256), F32),
            jax.ShapeDtypeStruct((all_rows, 256), F32),
            jax.ShapeDtypeStruct((all_rows, 256), BF16),
        ],
        scratch_shapes=[
            pltpu.VMEM((2, 2 * all_rows, LANES), BF16),
            pltpu.VMEM((2, 2 * all_rows, LANES), BF16),
            pltpu.VMEM((LANES, 2 * all_rows), BF16),
            pltpu.VMEM((2, 2 * all_rows, LANES), BF16),
            pltpu.VMEM((2, 2 * all_rows, LANES), BF16),
            pltpu.VMEM((2, 64, 2 * all_rows), F32),
            pltpu.VMEM((2, size, LANES), F32),
            pltpu.VMEM((2, size, LANES), F32),
        ],
        compiler_params=pltpu.CompilerParams(vmem_limit_bytes=VMEM_LIMIT),
        name="attend_back",
    )(place, queries, kv_own, kv_other, attended, inverse_total, attended_grad)
    dkv_got = swap(dkv_other, "col", 1)
    projected_grad, head_sums = pl.pallas_call(
        functools.partial(prepare_back_kernel, scale=scale),
        grid=(blocks,),
        in_specs=[
            tile(512), tile(LANES), tile(LANES), gain_spec, tile(256), tile(256), tile(256),
        ],
        out_specs=[tile(512), pl.BlockSpec((8, 3 * LANES), lambda i: (0, 0))],
        out_shape=[
            jax.ShapeDtypeStruct((all_rows, 512), BF16),
            jax.ShapeDtypeStruct((8, 3 * LANES), F32),
        ],
        name="prepare_back",
    )(projected, cos_table, sin_table, head_gains, dq, dkv_own, dkv_got)
    normed_one_grad = scatter_row(chunks(dot_nt(projected_grad, w_qkv).astype(BF16)))
    qkv_grad = fold_rows(dot_tn(normed_one_all, projected_grad))
    qkv_grad, o_grad, up_weight_grad = lax.optimization_barrier((qkv_grad, o_grad, up_weight_grad))
    qkv_grad, o_grad = lax.psum((qkv_grad, o_grad), "dp")
    input_part, attn_gain_grad = norm_backward(inputs, inverse_one, gain_one, normed_one_grad)
    input_grad = residual_grad + input_part
    input_grad = from_whole(
        input_grad[:, :width], swap(input_grad[:, width:].astype(BF16), "col", 1).astype(F32)
    )

    head_sums = head_sums[0].reshape(6, head)
    q_sum, k_sum = jnp.sum(head_sums[:4], axis=0), jnp.sum(head_sums[4:], axis=0)
    small = jnp.concatenate([attn_gain_grad[:width], ffn_gain_grad[:width], q_sum, k_sum])
    given = jnp.concatenate([attn_gain_grad[width:], ffn_gain_grad[width:], q_sum, k_sum])
    small = small + swap(given, "col", 1)
    for axis in ("row", "dp"):
        distance = 1
        while distance < lax.axis_size(axis):
            small = small + swap(small, axis, distance)
            distance *= 2
    attn_gain_grad, ffn_gain_grad = small[:width], small[width : 2 * width]
    q_gain_grad, k_gain_grad = small[2 * width : 2 * width + head], small[2 * width + head :]
    query_cols, kv_cols = q_weight.shape[1], k_weight.shape[1]
    qkv_grad = qkv_grad.astype(F32)
    return (
        output,
        input_grad,
        attn_gain_grad,
        qkv_grad[:, :query_cols],
        qkv_grad[:, query_cols : query_cols + kv_cols],
        qkv_grad[:, query_cols + kv_cols :],
        q_gain_grad,
        k_gain_grad,
        o_grad.astype(F32),
        ffn_gain_grad,
        gate_weight_grad.astype(F32),
        up_weight_grad.astype(F32),
        down_grad.astype(F32),
    )


def solution(mesh):
    in_specs = (
        P(("dp", "row"), "col"),
        P("dp", None),
        P("col"),
        P("col", "row"),
        P("col", "row"),
        P("col", "row"),
        P(),
        P(),
        P("row", "col"),
        P("col"),
        P("col", "row"),
        P("col", "row"),
        P("row", "col"),
        P(("dp", "row"), "col"),
    )
    out_specs = (
        P(("dp", "row"), "col"),
        P(("dp", "row"), "col"),
        P("col"),
        P("col", "row"),
        P("col", "row"),
        P("col", "row"),
        P(),
        P(),
        P("row", "col"),
        P("col"),
        P("col", "row"),
        P("col", "row"),
        P("row", "col"),
    )
    return jax.shard_map(body, mesh=mesh, in_specs=in_specs, out_specs=out_specs, check_vma=False)
```

```python
import functools

import jax
import jax.numpy as jnp
from jax import lax
from jax.experimental import pallas as pl
from jax.experimental.pallas import tpu as pltpu
from jax.sharding import PartitionSpec as P

EPSILON = 1e-05
ROPE_BASE = 1000000.0
MASKED_SCORE = -1e30
F32 = jnp.float32
BF16 = jnp.bfloat16
LANES = 128
VMEM_LIMIT = 56 * 1024 * 1024


def swap(values, axis, distance):
    count = lax.axis_size(axis)
    return lax.ppermute(values, axis, [(i, i ^ distance) for i in range(count)])


def dot(a, b):
    return jnp.dot(a, b, preferred_element_type=F32)


def dot_nt(a, b):
    return lax.dot_general(a, b, (((1,), (1,)), ((), ())), preferred_element_type=F32)


def dot_tn(a, b):
    return lax.dot_general(a, b, (((0,), (0,)), ((), ())), preferred_element_type=F32)


def gather_row(values):
    core = swap(values, "row", 1)
    far = swap(values, "row", 2)
    return [values, core, far, swap(far, "row", 1)]


def after(x, *others):
    return lax.optimization_barrier((x,) + others)[0]


def far_sum(parts):
    far = parts[2].astype(F32) + swap(parts[3], "row", 1).astype(F32)
    return far.astype(BF16)


def scatter_row(parts, far):
    far = swap(far, "row", 2)
    near = parts[0].astype(F32) + swap(parts[1], "row", 1).astype(F32)
    return near + far.astype(F32)


def sum_dp(values):
    count, me = lax.axis_size("dp"), lax.axis_index("dp")
    part = values.shape[0] // count

    def piece(k):
        return lax.dynamic_slice_in_dim(values, (me ^ k) * part, part)

    total = piece(0).astype(F32)
    for k in range(1, count):
        total = total + swap(piece(k), "dp", k).astype(F32)
    total = total.astype(BF16)
    result = jnp.zeros_like(values)
    for k in range(count):
        got = total if k == 0 else swap(total, "dp", k)
        result = lax.dynamic_update_slice_in_dim(result, got, (me ^ k) * part, 0)
    return result


def exchange_row(parts):
    return [parts[0]] + [swap(parts[k], "row", k) for k in (1, 2, 3)]


def sub_block(idx, col):
    return jnp.where(col == 0, 3 * idx, 1 + idx)


def natural_block(i, row, col):
    return 4 * ((i >> 1) ^ row) + sub_block(i & 1, col)


def own_before(block, col):
    sub = block & 3
    first = (sub > 0).astype(jnp.int32)
    second = (sub > 1).astype(jnp.int32) + (sub > 2).astype(jnp.int32)
    return 2 * (block >> 2) + jnp.where(col == 0, first, second)


def lane_of(rows):
    return lax.broadcasted_iota(jnp.int32, (rows, LANES), 1)


def second_sequence(block, size, boundary):
    token = block * size + lax.broadcasted_iota(jnp.int32, (size, LANES), 0)
    return token >= boundary


def half_pick(chunk, which):
    return chunk if which == 0 else pltpu.roll(chunk, 64, 1)


def query_pieces(queries, block, size, boundary, pair):
    lane = lane_of(size)
    second = second_sequence(block, size, boundary)
    extra = jnp.where(lane == 64, jnp.where(second, 0.0, 1.0), jnp.where(second, 1.0, 0.0))
    extra = jnp.where(lane <= 65, extra, 0.0)
    chunk = queries[:, pair * LANES : (pair + 1) * LANES].astype(F32)
    return jnp.concatenate(
        [jnp.where(lane < 64, half_pick(chunk, w), extra).astype(BF16) for w in (0, 1)], axis=0
    )


def build_keys(kv, block, size, boundary, g):
    lane = lane_of(size)
    second = second_sequence(block, size, boundary)
    extra = jnp.where(
        lane == 64,
        jnp.where(second, MASKED_SCORE, 0.0),
        jnp.where(second, 0.0, MASKED_SCORE),
    )
    extra = jnp.where(lane <= 65, extra, 0.0)
    ones = jnp.where(lane <= 65, 1.0, 0.0)
    key = jnp.where(lane < 64, half_pick(kv[:, :LANES], g), extra)
    value = jnp.where(lane < 64, half_pick(kv[:, LANES:], g), ones)
    return key.astype(BF16), value.astype(BF16)


def fill_keys(kv_refs, key_ref, value_ref, turned_ref, row, col, boundary, size):
    def step(n, carry):
        rows = pl.ds(pl.multiple_of(n * size, size), size)
        for k, ref in enumerate(kv_refs):
            kv = ref[rows, :].astype(F32)
            i = 2 * k + n
            target = pl.ds(pl.multiple_of(i * size, size), size)
            for g in range(2):
                key, value = build_keys(kv, natural_block(i, row, col), size, boundary, g)
                key_ref[g, target, :] = key
                value_ref[g, target, :] = value
            if turned_ref is not None:
                turned_ref[:, target] = kv[:, :LANES].T.astype(BF16)
        return carry

    lax.fori_loop(0, 2, step, 0)


def storage_of(n, row, size):
    return pl.multiple_of(((((n >> 1) ^ row) << 1) + (n & 1)) * size, size)


def attention_forward(place, q_ref, *refs, size, blocks):
    own_refs, other_refs, out_refs = refs[:4], refs[4:8], refs[8:12]
    inverse_ref, key_ref, value_ref, other_key_ref, other_value_ref = refs[12:]
    row, col, boundary = place[0], place[1], place[2]
    fill_keys(own_refs, key_ref, value_ref, None, row, col, boundary, size)
    fill_keys(other_refs, other_key_ref, other_value_ref, None, row, 1 - col, boundary, size)
    later = lax.broadcasted_iota(jnp.int32, (2 * size, size), 0) % size
    allowed = lax.broadcasted_iota(jnp.int32, (2 * size, size), 1) <= later
    lane = lane_of(size)

    def one_block(k, n, carry):
        i = 2 * k + n
        rows = pl.ds(pl.multiple_of(i * size, size), size)
        block = natural_block(i, row, col)
        queries = q_ref[rows, :]
        packed = [query_pieces(queries, block, size, boundary, g) for g in range(2)]

        def term(keys_from, values_from, start, g, diagonal):
            keys = pl.ds(start, size)
            weights = jnp.exp(dot_nt(packed[g], keys_from[g, keys, :]))
            if diagonal:
                weights = jnp.where(allowed, weights, 0.0)
            return dot(weights.astype(BF16), values_from[g, keys, :])

        def step(keys_from, values_from, m, sums):
            start = storage_of(m, row, size)
            return tuple(
                sums[g] + term(keys_from, values_from, start, g, False) for g in range(2)
            )

        first = jnp.where(block * size >= boundary, boundary // size, 0)
        start = pl.multiple_of(i * size, size)
        sums = tuple(term(key_ref, value_ref, start, g, True) for g in range(2))
        for part, sources in enumerate(((key_ref, value_ref), (other_key_ref, other_value_ref))):
            begin, end = own_before(first, col ^ part), own_before(block, col ^ part)
            sums = lax.fori_loop(begin, end, functools.partial(step, *sources), sums)
        for g in range(2):
            inverse = 1.0 / sums[g][:, 64:65]
            scaled = sums[g] * inverse
            columns = slice(g * LANES, (g + 1) * LANES)
            joined = jnp.where(lane < 64, scaled[:size], pltpu.roll(scaled[size:], 64, 1))
            out_refs[k][pl.ds(pl.multiple_of(n * size, size), size), columns] = joined.astype(BF16)
            inverse_ref[rows, columns] = jnp.where(lane < 64, inverse[:size], inverse[size:])
        return carry

    for k in range(4):
        lax.fori_loop(0, 2, functools.partial(one_block, k), 0)


def attention_backward(place, q_ref, *refs, size, blocks, part):
    kv_refs, out_refs, inverse_ref, grad_refs = refs[:4], refs[4:8], refs[8], refs[9:13]
    if part == 1:
        dkv_ref, dq_sum = refs[13:15]
    else:
        earlier_ref, dkv_ref, dq_ref, dq_sum = refs[13:17]
    key_ref, value_ref, turned_ref, packed_ref, packed_grad_ref, dk_sum, dv_sum = refs[-7:]
    row, col, boundary = place[0], place[1], place[2]
    lane = lane_of(size)
    fill_keys(kv_refs, key_ref, value_ref, turned_ref, row, col ^ part, boundary, size)

    def fill(k, n, carry):
        i = 2 * k + n
        rows = pl.ds(pl.multiple_of(i * size, size), size)
        inner = pl.ds(pl.multiple_of(n * size, size), size)
        block = natural_block(i, row, col)
        wide = pl.ds(pl.multiple_of(i * 2 * size, 2 * size), 2 * size)
        queries = q_ref[rows, :]
        for g in range(2):
            columns = slice(g * LANES, (g + 1) * LANES)
            packed_ref[g, wide, :] = query_pieces(queries, block, size, boundary, g)
            scaled = grad_refs[k][inner, columns].astype(F32) * inverse_ref[rows, columns]
            product = scaled * out_refs[k][inner, columns].astype(F32)
            pieces = []
            for w in (0, 1):
                total = -jnp.sum(
                    jnp.where((lane >= 64) if w else (lane < 64), product, 0.0), axis=1, keepdims=True
                )
                high = total.astype(BF16).astype(F32)
                extra = jnp.where(lane == 64, high, jnp.where(lane == 65, total - high, 0.0))
                pieces.append(jnp.where(lane < 64, half_pick(scaled, w), extra).astype(BF16))
            packed_grad_ref[g, wide, :] = jnp.concatenate(pieces, axis=0)
            if part == 1:
                dq_sum[g, :, wide] = jnp.zeros((64, 2 * size), F32)
            else:
                dq_sum[g, :, wide] = earlier_ref[g, :, wide]
        return carry

    for k in range(4):
        lax.fori_loop(0, 2, functools.partial(fill, k), 0)
    later = lax.broadcasted_iota(jnp.int32, (size, 2 * size), 1) % size
    allowed = lax.broadcasted_iota(jnp.int32, (size, 2 * size), 0) <= later

    def pair(start, i, diagonal):
        keys = pl.ds(start, size)
        wide = pl.ds(pl.multiple_of(i * 2 * size, 2 * size), 2 * size)
        for g in range(2):
            queries = packed_ref[g, wide, :]
            grads = packed_grad_ref[g, wide, :]
            weights = jnp.exp(dot_nt(key_ref[g, keys, :], queries))
            if diagonal:
                weights = jnp.where(allowed, weights, 0.0)
            change = dot_nt(value_ref[g, keys, :], grads)
            score = (weights * change).astype(BF16)
            value_term = dot(weights.astype(BF16), grads)
            key_term = dot(score, queries)
            if diagonal:
                dv_sum[g] = value_term
                dk_sum[g] = key_term
            else:
                dv_sum[g] += value_term
                dk_sum[g] += key_term
            dq_sum[g, :, wide] += dot(turned_ref[64 * g : 64 * (g + 1), keys], score)

    def one_block(i, carry):
        block = natural_block(i, row, col ^ part)
        start = pl.multiple_of(i * size, size)
        last = jnp.where((block + 1) * size <= boundary, (boundary - 1) // size, 2 * blocks - 1)
        begin = own_before(block, col) + 1 - part
        end = own_before(last + 1, col)
        if part == 0:
            pair(start, i, True)
        else:
            dk_sum[...] = jnp.zeros_like(dk_sum)
            dv_sum[...] = jnp.zeros_like(dv_sum)

        def step(n, carry):
            pair(start, (((n >> 1) ^ row) << 1) + (n & 1), False)
            return carry

        lax.fori_loop(begin, end, step, 0)
        rows = pl.ds(start, size)
        kind = dkv_ref.dtype
        key_grad = jnp.where(lane < 64, dk_sum[0], pltpu.roll(dk_sum[1], 64, 1))
        value_grad = jnp.where(lane < 64, dv_sum[0], pltpu.roll(dv_sum[1], 64, 1))
        dkv_ref[rows, :LANES] = key_grad.astype(kind)
        dkv_ref[rows, LANES:] = value_grad.astype(kind)
        return carry

    lax.fori_loop(0, blocks, one_block, 0)
    if part == 1:
        return

    def finish(i, carry):
        rows = pl.ds(pl.multiple_of(i * size, size), size)
        for g in range(2):
            wide = pl.multiple_of(i * 2 * size, 2 * size)
            stacked = jnp.concatenate(
                [dq_sum[g, :, pl.ds(wide, size)], dq_sum[g, :, pl.ds(wide + size, size)]], axis=0
            )
            dq_ref[rows, g * LANES : (g + 1) * LANES] = stacked.T
        return carry

    lax.fori_loop(0, blocks, finish, 0)


def head_totals(values):
    a = lax.broadcasted_iota(jnp.int32, (LANES, LANES), 0) // 64
    b = lax.broadcasted_iota(jnp.int32, (LANES, LANES), 1) // 64
    same = jnp.where(a == b, 1.0, 0.0).astype(BF16)
    high = values.astype(BF16)
    low = (values - high.astype(F32)).astype(BF16)
    return dot(high, same) + dot(low, same)


def turned_lanes(values):
    first = lane_of(values.shape[0]) % 64 < 32
    return jnp.where(first, pltpu.roll(values, LANES - 32, 1), pltpu.roll(values, 32, 1))


def prepare_kernel(
    left_ref, right_ref, w_mine, w_got, cos_ref, sin_ref, gain_ref, wide_gain_ref, *refs, scale, width
):
    q_ref, kv_ref, pre_ref, normed_ref = refs[-4:]
    left, right = left_ref[...].astype(F32), right_ref[...].astype(F32)
    squares = jnp.sum(left * left, axis=1, keepdims=True) + jnp.sum(
        right * right, axis=1, keepdims=True
    )
    inverse = lax.rsqrt(squares / (2 * width) + EPSILON)
    left = (left * inverse * wide_gain_ref[:, :width]).astype(BF16)
    right = (right * inverse * wide_gain_ref[:, width:]).astype(BF16)
    normed_ref[:, :width] = left
    normed_ref[:, width:] = right
    pre = dot(left, w_mine[...]) + dot(right, w_got[...])
    pre_ref[...] = pre[:, : 3 * LANES]
    for n in range(3):
        values = pre[:, n * LANES : (n + 1) * LANES]
        inverse = lax.rsqrt(head_totals(values * values) / 64 + EPSILON)
        normed = values * inverse * gain_ref[(0 if n < 2 else 1) : (1 if n < 2 else 2), :]
        rotated = normed * cos_ref[...] + turned_lanes(normed) * sin_ref[...]
        if n < 2:
            q_ref[:, n * LANES : (n + 1) * LANES] = (
                rotated.astype(BF16).astype(F32) * scale
            ).astype(BF16)
        else:
            kv_ref[:, :LANES] = rotated.astype(BF16)
    kv_ref[:, LANES:] = pre[:, 3 * LANES :].astype(BF16)


def prepare_back_kernel(
    pre_ref,
    cos_ref,
    sin_ref,
    gain_ref,
    dq_ref,
    own_ref,
    got_ref,
    w_mine,
    w_got,
    normed_ref,
    *refs,
    scale,
    width,
):
    out_ref, sums_ref, gain_sums_ref, grad_out_ref = refs[-4:]

    @pl.when(pl.program_id(0) == 0)
    def _():
        sums_ref[...] = jnp.zeros_like(sums_ref)
        gain_sums_ref[...] = jnp.zeros_like(gain_sums_ref)

    pieces = []
    for n in range(3):
        columns = slice(n * LANES, (n + 1) * LANES)
        values = pre_ref[:, columns]
        inverse = lax.rsqrt(head_totals(values * values) / 64 + EPSILON)
        if n < 2:
            grad = dq_ref[:, columns] * scale
        else:
            grad = own_ref[:, :LANES] + got_ref[:, :LANES].astype(F32)
        grad = grad * cos_ref[...] - turned_lanes(grad) * sin_ref[...]
        hat = values * inverse
        sums_ref[0:1, columns] += jnp.sum(grad * hat, axis=0, keepdims=True)
        scaled = grad * gain_ref[(0 if n < 2 else 1) : (1 if n < 2 else 2), :]
        mean = head_totals(scaled * hat) / 64
        pieces.append((inverse * (scaled - hat * mean)).astype(BF16))
    pieces.append((own_ref[:, LANES:] + got_ref[:, LANES:].astype(F32)).astype(BF16))
    grads = jnp.concatenate(pieces, axis=1)
    out_ref[...] = grads
    for half, w_ref in enumerate((w_mine, w_got)):
        columns = slice(half * width, (half + 1) * width)
        term = dot_nt(grads, w_ref[...])
        grad_out_ref[:, columns] = term.astype(BF16)
        product = term * normed_ref[:, columns].astype(F32)
        gain_sums_ref[0:1, columns] += jnp.sum(product, axis=0, keepdims=True)


def feed_forward_kernel(
    x_one, x_two, left_one, left_two, right_one, right_two,
    gate_mine, gate_got, up_mine, up_got, down_mine, down_got, *refs, width,
):
    hidden_ref, gate_grad_ref, up_grad_ref, x_out_ref, cot_out_ref = refs[-8:-3]
    back_one, back_two, total = refs[-3:]
    step = hidden_ref.shape[1]
    x = jnp.concatenate([x_one[...], x_two[...]], axis=0)
    left = jnp.concatenate([left_one[...], left_two[...]], axis=0)
    right = jnp.concatenate([right_one[...], right_two[...]], axis=0)

    @pl.when(pl.program_id(0) == 0)
    def _():
        x_out_ref[...] = x
        cot_out_ref[:, :width] = left
        cot_out_ref[:, width:] = right

    mine = jnp.concatenate([gate_mine[...], up_mine[...]], axis=1)
    got = jnp.concatenate([gate_got[...], up_got[...]], axis=1)
    both = dot(x[:, :width], mine) + dot(x[:, width:], got)
    gate, up = both[:, :step], both[:, step:]
    grad = dot_nt(left, down_mine[...]) + dot_nt(right, down_got[...])
    sigmoid = 1.0 / (1.0 + jnp.exp(-gate))
    silu = gate * sigmoid
    hidden_ref[...] = (silu * up).astype(BF16)
    gate_grad = (grad * up * (sigmoid + silu * (1.0 - sigmoid))).astype(BF16)
    up_grad = (grad * silu).astype(BF16)
    gate_grad_ref[...] = gate_grad
    up_grad_ref[...] = up_grad
    grads = jnp.concatenate([gate_grad, up_grad], axis=1)
    one, two = dot_nt(grads, mine), dot_nt(grads, got)

    @pl.when(pl.program_id(0) == 0)
    def _():
        total[:, :width] = one
        total[:, width:] = two

    @pl.when(pl.program_id(0) > 0)
    def _():
        total[:, :width] += one
        total[:, width:] += two

    @pl.when(pl.program_id(0) == pl.num_programs(0) - 1)
    def _():
        rows = back_one.shape[0]
        back_one[...] = total[:rows, :].astype(BF16)
        back_two[...] = total[rows:, :].astype(BF16)


def norm_rows(values, gain):
    inverse = lax.rsqrt(jnp.mean(values * values, axis=1, keepdims=True) + EPSILON)
    return (values * inverse * gain).astype(BF16), inverse


def norm_backward(values, inverse, gain, grad):
    gain_grad = jnp.sum(grad * values * inverse, axis=0)
    scaled = grad * gain
    inner = jnp.mean(scaled * values, axis=1, keepdims=True)
    return scaled * inverse - values * (inverse * inverse * inverse * inner), gain_grad


def body(
    tokens,
    seq_lengths,
    attn_gain,
    q_weight,
    k_weight,
    v_weight,
    q_gain,
    k_gain,
    o_weight,
    ffn_gain,
    gate_weight,
    up_weight,
    down_weight,
    cotangent,
):
    row, col = lax.axis_index("row"), lax.axis_index("col")
    local_rows, width = tokens.shape
    size = local_rows // 4
    own_rows = 2 * size
    blocks = 8
    all_rows = blocks * size
    head = q_gain.shape[0]
    scale = head ** (-0.5)
    hidden_cols = gate_weight.shape[1]
    boundary = seq_lengths[0, 0]

    def mine(x):
        outer = jnp.concatenate([x[:size], x[3 * size :]], axis=0)
        inner = x[size : 3 * size]
        return jnp.where(col == 0, outer, inner), jnp.where(col == 0, inner, outer)

    def to_whole(x):
        keep, give = mine(x)
        return jnp.concatenate([keep, swap(give, "col", 1)], axis=1)

    def from_whole(keep, got):
        outer = jnp.where(col == 0, keep, got)
        inner = jnp.where(col == 0, got, keep)
        return jnp.concatenate([outer[:size], inner, outer[size:]], axis=0)

    def both(x, axis):
        return jnp.concatenate([x, swap(x, "col", 1)], axis=axis)

    def through_dp(x, anchor):
        part = x.shape[0] // lax.axis_size("dp")
        piece = lax.dynamic_slice_in_dim(x, lax.axis_index("dp") * part, part)
        return swap(after(piece, anchor), "col", 1)

    keep, give = mine(tokens)
    got = swap(give, "col", 1)
    w_mine = jnp.concatenate([q_weight, k_weight, v_weight], axis=1)
    w_got = swap(after(w_mine, got), "col", 1)
    gains = both(jnp.stack([attn_gain, ffn_gain]), 1)

    index = jnp.arange(all_rows, dtype=jnp.int32)
    token = natural_block(index // size, row, col) * size + index % size
    position = jnp.where(token >= boundary, token - boundary, token)
    lane = jnp.arange(LANES, dtype=jnp.int32)
    frequency = ROPE_BASE ** (-((jnp.arange(head // 2, dtype=F32)) * 2.0) / head)
    angle = position.astype(F32)[:, None] * frequency[None, :]
    cos_table = jnp.tile(jnp.cos(angle), (1, LANES // (head // 2)))
    sin_table = jnp.tile(jnp.sin(angle), (1, LANES // (head // 2)))
    sin_table = jnp.where((lane % head < head // 2)[None, :], -sin_table, sin_table)
    head_gains = jnp.stack([jnp.tile(q_gain, 2), jnp.tile(k_gain, 2)])

    got, cos_table, sin_table, gains = lax.optimization_barrier(
        (got, cos_table, sin_table, gains)
    )
    gain_one, gain_two = gains[0], gains[1]
    left, right = gather_row(keep), gather_row(got)
    inputs = jnp.concatenate([keep, got], axis=1).astype(F32)
    inverse_one = lax.rsqrt(jnp.mean(inputs * inputs, axis=1, keepdims=True) + EPSILON)

    def tile(columns, first=0):
        return pl.BlockSpec((size, columns), lambda i: (i + first, 0))

    def fixed(x):
        return pl.BlockSpec(x.shape, lambda i: (0, 0))

    def rows_of(count, columns, kind):
        return jax.ShapeDtypeStruct((count, columns), kind)

    anywhere = pl.BlockSpec(memory_space=pl.ANY)
    params = pltpu.CompilerParams(vmem_limit_bytes=VMEM_LIMIT)
    wide_gain = gain_one[None, :]

    def prepare(k, earlier):
        return pl.pallas_call(
            functools.partial(prepare_kernel, scale=scale, width=width),
            grid=(2,),
            in_specs=[tile(width), tile(width), fixed(w_mine), fixed(w_got)]
            + [tile(LANES, 2 * k)] * 2
            + [fixed(head_gains), fixed(wide_gain)]
            + [anywhere] * len(earlier),
            out_specs=[tile(256, 2 * k), tile(256), tile(384, 2 * k), tile(2 * width, 2 * k)],
            out_shape=[
                rows_of(all_rows, 256, BF16),
                rows_of(own_rows, 256, BF16),
                rows_of(all_rows, 384, F32),
                rows_of(all_rows, 2 * width, BF16),
            ],
            input_output_aliases={8 + n: m for n, m in enumerate((0, 2, 3)[: len(earlier)])},
            compiler_params=params,
            name="prepare",
        )(
            left[k], right[k], w_mine, w_got, cos_table, sin_table, head_gains, wide_gain, *earlier
        )

    kept, kv_own, kv_other = (), [], []
    for k in range(4):
        if k == 1:
            o_other = swap(after(o_weight, w_got), "col", 1)
            down_piece = through_dp(down_weight, w_got)
            left[1], o_other, down_piece = lax.optimization_barrier((left[1], o_other, down_piece))
            down_got = lax.all_gather(down_piece, "dp", axis=0, tiled=True)
            cot_keep, cot_give = mine(cotangent)
            cot_left = gather_row(after(cot_keep, kv_own[0]))
        if k == 3:
            left[3], kv_other[0], kv_other[1], cot_left[2] = lax.optimization_barrier(
                (left[3], kv_other[0], kv_other[1], cot_left[2])
            )
        queries, kv, pre, normed_one_all = prepare(k, kept)
        kept = (queries, pre, normed_one_all)
        kv_own.append(kv)
        kv_other.append(swap(kv, "col", 1))


    place = jnp.stack([row.astype(jnp.int32), col.astype(jnp.int32), boundary.astype(jnp.int32)])
    whole = pl.BlockSpec(memory_space=pltpu.VMEM)
    smem = pl.BlockSpec(memory_space=pltpu.SMEM)
    key_scratch = [pltpu.VMEM((2, all_rows, LANES), BF16)] * 2
    gate_up_give = jnp.concatenate([gate_weight, up_weight], axis=1)
    gate_up_got = swap(after(gate_up_give, kv_other[2], kv_other[3]), "col", 1)
    cot_got = swap(after(cot_give, kv_other[2], kv_other[3]), "col", 1)
    queries_in, down_got = lax.optimization_barrier((queries, down_got))
    *attended, inverse_total = pl.pallas_call(
        functools.partial(attention_forward, size=size, blocks=blocks),
        in_specs=[smem] + [whole] * 9,
        out_specs=[whole] * 5,
        out_shape=[rows_of(own_rows, 256, BF16)] * 4 + [rows_of(all_rows, 256, F32)],
        scratch_shapes=key_scratch * 2,
        compiler_params=params,
        name="attend",
    )(place, queries_in, *kv_own, *kv_other)

    w_o = jnp.concatenate(gather_row(jnp.concatenate([o_weight, o_other], axis=1)), axis=0)
    attended_own = jnp.concatenate(exchange_row(attended), axis=1)
    attended_own, gate_up_got = lax.optimization_barrier((attended_own, gate_up_got))
    residual = inputs + dot(attended_own, w_o)
    normed_two, inverse_two = norm_rows(residual, gain_two)
    cot_own = jnp.concatenate([cot_keep, cot_got], axis=1)
    cot_right = [cot_got, swap(cot_got, "row", 1), swap(after(cot_got, attended_own), "row", 2)]
    gathered = [normed_two, swap(normed_two, "row", 1), swap(normed_two, "row", 2)]
    hidden_cols = gate_weight.shape[1]
    ffn_weights = (gate_weight, gate_up_got, up_weight, gate_up_got, down_weight, down_got)
    hidden_step = hidden_cols // 3

    def feed_forward(pair, earlier):
        def part(rows, columns, fixed_row=0):
            return pl.BlockSpec((rows, columns), lambda i: (fixed_row, i))

        def still(rows, columns, fixed_row=0):
            return pl.BlockSpec((rows, columns), lambda i: (fixed_row, 0))

        down_spec = pl.BlockSpec((hidden_step, width), lambda i: (i, 0))
        ks = (2 * pair, 2 * pair + 1)
        return pl.pallas_call(
            functools.partial(feed_forward_kernel, width=width),
            grid=(3,),
            in_specs=[still(own_rows, 2 * width)] * 2
            + [still(own_rows, width)] * 4
            + [part(width, hidden_step)] * 3
            + [pl.BlockSpec((width, hidden_step), lambda i: (0, i + 3))]
            + [down_spec] * 2
            + [anywhere] * len(earlier),
            out_specs=[part(2 * own_rows, hidden_step, pair)] * 3
            + [still(2 * own_rows, 2 * width, pair)] * 2
            + [still(own_rows, 2 * width)] * 2,
            out_shape=[rows_of(all_rows, hidden_cols, BF16)] * 3
            + [rows_of(all_rows, 2 * width, BF16)] * 2
            + [rows_of(own_rows, 2 * width, BF16)] * 2,
            scratch_shapes=[pltpu.VMEM((2 * own_rows, 2 * width), F32)],
            input_output_aliases={12 + n: n for n in range(len(earlier))},
            compiler_params=params,
            name="feed_forward",
        )(
            *[gathered[k] for k in ks],
            *[cot_left[k] for k in ks],
            *[cot_right[k] for k in ks],
            *ffn_weights,
            *earlier,
        )

    *kept, back_0, back_1 = feed_forward(0, ())
    gathered.append(swap(after(gathered[2], back_0), "row", 1))
    cot_right.append(swap(after(cot_right[2], back_0), "row", 1))
    *kept, back_2, back_3 = feed_forward(1, kept)
    hidden, gate_grad, up_grad, normed_two_all, cot_all = kept
    backs = [back_0, back_1, back_2, back_3]
    back_far = far_sum(backs)
    normed_two_grad = scatter_row(backs, back_far)

    hidden_late, normed_late = after(hidden, back_far), after(normed_two_all, back_far)
    down_give = dot_tn(hidden, cot_all[:, width:]).astype(BF16)
    gate_give = dot_tn(normed_late[:, width:], gate_grad).astype(BF16)
    up_give = dot_tn(normed_late[:, width:], up_grad).astype(BF16)
    ffn_out = [
        jnp.concatenate([dot(part, down_weight), dot(part, down_got)], axis=1).astype(BF16)
        for part in [hidden_late[k * own_rows : (k + 1) * own_rows] for k in range(4)]
    ]
    down_other, gate_other, up_other = [swap(x, "col", 1) for x in (down_give, gate_give, up_give)]
    normed_two_grad, *ffn_out = lax.optimization_barrier((normed_two_grad, *ffn_out))
    residual_part, ffn_gain_grad = norm_backward(residual, inverse_two, gain_two, normed_two_grad)
    residual_grad = cot_own.astype(F32) + residual_part
    branch_grad = residual_grad.astype(BF16)
    attended_grad = dot_nt(branch_grad, w_o).astype(BF16)
    attended_grad = exchange_row([attended_grad[:, k * 256 : (k + 1) * 256] for k in range(4)])

    def add_other(keep, other):
        return (keep + other.astype(F32)).astype(BF16)

    down_grad = add_other(dot_tn(hidden, cot_all[:, :width]), down_other)
    gate_keep = dot_tn(normed_late[:, :width], gate_grad)
    up_keep = dot_tn(normed_late[:, :width], up_grad)
    down_grad = lax.psum_scatter(down_grad, "dp", scatter_dimension=0, tiled=True)
    down_grad, gate_keep, up_keep, *attended_grad = lax.optimization_barrier(
        (down_grad, gate_keep, up_keep, *attended_grad)
    )
    down_grad = lax.all_gather(down_grad, "dp", axis=0, tiled=True)

    ffn_out = scatter_row(ffn_out, after(far_sum(ffn_out), attended_grad[3]))
    output = (residual + ffn_out).astype(BF16)
    output = from_whole(output[:, :width], swap(output[:, width:], "col", 1))

    o_give = dot_tn(attended_own, branch_grad[:, width:]).astype(BF16)
    o_other = swap(o_give, "col", 1)
    o_rows = o_weight.shape[0]
    def attend_back(part, kv_parts, earlier):
        dq_shape = jax.ShapeDtypeStruct((2, 64, 2 * all_rows), F32)
        if part == 1:
            shapes, extra = [rows_of(all_rows, 256, BF16), dq_shape], []
        else:
            shapes = [rows_of(all_rows, 256, F32), rows_of(all_rows, 256, F32)]
            extra = [pltpu.VMEM(dq_shape.shape, F32)]
        return pl.pallas_call(
            functools.partial(attention_backward, size=size, blocks=blocks, part=part),
            in_specs=[smem] + [whole] * (14 + len(earlier)),
            out_specs=[whole] * 2,
            out_shape=shapes,
            scratch_shapes=extra
            + key_scratch
            + [
                pltpu.VMEM((LANES, all_rows), BF16),
                pltpu.VMEM((2, 2 * all_rows, LANES), BF16),
                pltpu.VMEM((2, 2 * all_rows, LANES), BF16),
                pltpu.VMEM((2, size, LANES), F32),
                pltpu.VMEM((2, size, LANES), F32),
            ],
            compiler_params=params,
            name="attend_back",
        )(place, queries, *kv_parts, *attended, inverse_total, *attended_grad, *earlier)

    dkv_other, dq_part = attend_back(1, kv_other, ())
    dkv_got = swap(dkv_other, "col", 1)
    gate_weight_grad = add_other(gate_keep, after(gate_other, dq_part))
    up_weight_grad = add_other(up_keep, after(up_other, dq_part))
    gate_up_grad = jnp.concatenate([gate_weight_grad, up_weight_grad], axis=1)
    dq_part, gate_up_grad, down_grad = lax.optimization_barrier((dq_part, gate_up_grad, down_grad))
    gate_up_grad = lax.psum_scatter(gate_up_grad, "dp", scatter_dimension=0, tiled=True)
    dkv_own, dq = attend_back(0, kv_own, (dq_part,))
    o_grad = add_other(dot_tn(attended_own, branch_grad[:, :width]), after(o_other, dq))
    o_grad = [o_grad[k * o_rows : (k + 1) * o_rows] for k in range(4)]
    o_grad = scatter_row(o_grad, far_sum(o_grad)).astype(BF16)

    def prepare_back(k, earlier):
        return pl.pallas_call(
            functools.partial(prepare_back_kernel, scale=scale, width=width),
            grid=(2,),
            in_specs=[tile(384, 2 * k), tile(LANES, 2 * k), tile(LANES, 2 * k), fixed(head_gains)]
            + [tile(256, 2 * k)] * 3
            + [fixed(w_mine), fixed(w_got), tile(2 * width, 2 * k)]
            + [anywhere] * len(earlier),
            out_specs=[
                tile(512, 2 * k),
                pl.BlockSpec((8, 3 * LANES), lambda i: (0, 0)),
                pl.BlockSpec((8, 2 * width), lambda i: (0, 0)),
                tile(2 * width),
            ],
            out_shape=[
                rows_of(all_rows, 512, BF16),
                rows_of(8, 3 * LANES, F32),
                rows_of(8, 2 * width, F32),
                rows_of(own_rows, 2 * width, BF16),
            ],
            input_output_aliases={10: 0} if earlier else {},
            compiler_params=params,
            name="prepare_back",
        )(
            pre, cos_table, sin_table, head_gains, dq, dkv_own, dkv_got, w_mine, w_got,
            normed_one_all, *earlier
        )

    kept, head_sums, gain_sums, backs = (), 0.0, 0.0, [None] * 4
    for k in (3, 2, 1, 0):
        projected_grad, one, two, backs[k] = prepare_back(k, kept)
        head_sums, gain_sums = head_sums + one, gain_sums + two
        if k == 2:
            back_far = far_sum(backs)
            projected_grad, back_far = lax.optimization_barrier((projected_grad, back_far))
        if k == 1:
            projected_grad, gate_up_grad = lax.optimization_barrier((projected_grad, gate_up_grad))
            gate_up_grad = lax.all_gather(gate_up_grad, "dp", axis=0, tiled=True)
        kept = (projected_grad,)
    normed_one_grad = scatter_row(backs, back_far)
    normed_one_grad, normed_one_all, gate_up_grad, output = lax.optimization_barrier(
        (normed_one_grad, normed_one_all, gate_up_grad, output)
    )
    attn_gain_grad = gain_sums[0] / gain_one
    qkv_other = swap(dot_tn(normed_one_all[:, width:], projected_grad).astype(BF16), "col", 1)
    qkv_grad = add_other(dot_tn(normed_one_all[:, :width], projected_grad), qkv_other)
    qkv_rows = qkv_grad.shape[0]
    joined = sum_dp(jnp.concatenate([qkv_grad, o_grad], axis=0))
    qkv_grad, o_grad = joined[:qkv_rows], joined[qkv_rows:]
    input_part, _ = norm_backward(inputs, inverse_one, gain_one, normed_one_grad)
    input_grad = residual_grad + input_part
    input_grad = from_whole(
        input_grad[:, :width], swap(after(input_grad[:, width:].astype(BF16), qkv_other), "col", 1).astype(F32)
    )

    head_sums = head_sums[0].reshape(6, head)
    q_sum, k_sum = jnp.sum(head_sums[:4], axis=0), jnp.sum(head_sums[4:], axis=0)
    small = jnp.concatenate([attn_gain_grad[:width], ffn_gain_grad[:width], q_sum, k_sum])
    given = jnp.concatenate([attn_gain_grad[width:], ffn_gain_grad[width:], q_sum, k_sum])
    small, given = after(small, normed_one_grad), after(given, normed_one_grad)
    small = small + swap(given, "col", 1)
    for axis in ("row", "dp"):
        distance = 1
        while distance < lax.axis_size(axis):
            small = small + swap(small, axis, distance)
            distance *= 2
    attn_gain_grad, ffn_gain_grad = small[:width], small[width : 2 * width]
    q_gain_grad, k_gain_grad = small[2 * width : 2 * width + head], small[2 * width + head :]
    query_cols, kv_cols = q_weight.shape[1], k_weight.shape[1]
    qkv_grad = qkv_grad.astype(F32)
    return (
        output,
        input_grad,
        attn_gain_grad,
        qkv_grad[:, :query_cols],
        qkv_grad[:, query_cols : query_cols + kv_cols],
        qkv_grad[:, query_cols + kv_cols :],
        q_gain_grad,
        k_gain_grad,
        o_grad.astype(F32),
        ffn_gain_grad,
        gate_up_grad[:, :hidden_cols].astype(F32),
        gate_up_grad[:, hidden_cols:].astype(F32),
        down_grad.astype(F32),
    )


def solution(mesh):
    in_specs = (
        P(("dp", "row"), "col"),
        P("dp", None),
        P("col"),
        P("col", "row"),
        P("col", "row"),
        P("col", "row"),
        P(),
        P(),
        P("row", "col"),
        P("col"),
        P("col", "row"),
        P("col", "row"),
        P("row", "col"),
        P(("dp", "row"), "col"),
    )
    out_specs = (
        P(("dp", "row"), "col"),
        P(("dp", "row"), "col"),
        P("col"),
        P("col", "row"),
        P("col", "row"),
        P("col", "row"),
        P(),
        P(),
        P("row", "col"),
        P("col"),
        P("col", "row"),
        P("col", "row"),
        P("row", "col"),
    )
    return jax.shard_map(body, mesh=mesh, in_specs=in_specs, out_specs=out_specs, check_vma=False)
```

```python
import functools

import jax
import jax.numpy as jnp
from jax import lax
from jax.experimental import pallas as pl
from jax.experimental.pallas import tpu as pltpu
from jax.sharding import PartitionSpec as P

EPSILON = 1e-05
ROPE_BASE = 1000000.0
MASKED_SCORE = -1e30
F32 = jnp.float32
BF16 = jnp.bfloat16
LANES = 128
VMEM_LIMIT = 56 * 1024 * 1024


def swap(values, axis, distance):
    count = lax.axis_size(axis)
    return lax.ppermute(values, axis, [(i, i ^ distance) for i in range(count)])


def dot(a, b):
    return jnp.dot(a, b, preferred_element_type=F32)


def dot_nt(a, b):
    return lax.dot_general(a, b, (((1,), (1,)), ((), ())), preferred_element_type=F32)


def dot_tn(a, b):
    return lax.dot_general(a, b, (((0,), (0,)), ((), ())), preferred_element_type=F32)


def gather_row(values):
    core = swap(values, "row", 1)
    far = swap(values, "row", 2)
    return [values, core, far, swap(far, "row", 1)]


def after(x, *others):
    return lax.optimization_barrier((x,) + others)[0]


def far_sum(parts):
    far = parts[2].astype(F32) + swap(parts[3], "row", 1).astype(F32)
    return far.astype(BF16)


def scatter_row(parts, far):
    far = swap(far, "row", 2)
    near = parts[0].astype(F32) + swap(parts[1], "row", 1).astype(F32)
    return near + far.astype(F32)


def sum_dp(values):
    count, me = lax.axis_size("dp"), lax.axis_index("dp")
    part = values.shape[0] // count

    def piece(k):
        return lax.dynamic_slice_in_dim(values, (me ^ k) * part, part)

    total = piece(0).astype(F32)
    for k in range(1, count):
        total = total + swap(piece(k), "dp", k).astype(F32)
    total = total.astype(BF16)
    result = jnp.zeros_like(values)
    for k in range(count):
        got = total if k == 0 else swap(total, "dp", k)
        result = lax.dynamic_update_slice_in_dim(result, got, (me ^ k) * part, 0)
    return result


def exchange_row(parts):
    return [parts[0]] + [swap(parts[k], "row", k) for k in (1, 2, 3)]


def sub_block(idx, col):
    return jnp.where(col == 0, 3 * idx, 1 + idx)


def natural_block(i, row, col):
    return 4 * ((i >> 1) ^ row) + sub_block(i & 1, col)


def own_before(block, col):
    sub = block & 3
    first = (sub > 0).astype(jnp.int32)
    second = (sub > 1).astype(jnp.int32) + (sub > 2).astype(jnp.int32)
    return 2 * (block >> 2) + jnp.where(col == 0, first, second)


def lane_of(rows):
    return lax.broadcasted_iota(jnp.int32, (rows, LANES), 1)


def second_sequence(block, size, boundary):
    token = block * size + lax.broadcasted_iota(jnp.int32, (size, LANES), 0)
    return token >= boundary


def half_pick(chunk, which):
    return chunk if which == 0 else pltpu.roll(chunk, 64, 1)


def query_pieces(queries, block, size, boundary, pair):
    lane = lane_of(size)
    second = second_sequence(block, size, boundary)
    extra = jnp.where(lane == 64, jnp.where(second, 0.0, 1.0), jnp.where(second, 1.0, 0.0))
    extra = jnp.where(lane <= 65, extra, 0.0)
    chunk = queries[:, pair * LANES : (pair + 1) * LANES].astype(F32)
    return jnp.concatenate(
        [jnp.where(lane < 64, half_pick(chunk, w), extra).astype(BF16) for w in (0, 1)], axis=0
    )


def build_keys(kv, block, size, boundary, g):
    lane = lane_of(size)
    second = second_sequence(block, size, boundary)
    extra = jnp.where(
        lane == 64,
        jnp.where(second, MASKED_SCORE, 0.0),
        jnp.where(second, 0.0, MASKED_SCORE),
    )
    extra = jnp.where(lane <= 65, extra, 0.0)
    ones = jnp.where(lane <= 65, 1.0, 0.0)
    key = jnp.where(lane < 64, half_pick(kv[:, :LANES], g), extra)
    value = jnp.where(lane < 64, half_pick(kv[:, LANES:], g), ones)
    return key.astype(BF16), value.astype(BF16)


def fill_keys(kv_refs, key_ref, value_ref, turned_ref, row, col, boundary, size):
    def step(n, carry):
        rows = pl.ds(pl.multiple_of(n * size, size), size)
        for k, ref in enumerate(kv_refs):
            kv = ref[rows, :].astype(F32)
            i = 2 * k + n
            target = pl.ds(pl.multiple_of(i * size, size), size)
            for g in range(2):
                key, value = build_keys(kv, natural_block(i, row, col), size, boundary, g)
                key_ref[g, target, :] = key
                value_ref[g, target, :] = value
            if turned_ref is not None:
                turned_ref[:, target] = kv[:, :LANES].T.astype(BF16)
        return carry

    lax.fori_loop(0, 2, step, 0)


def storage_of(n, row, size):
    return pl.multiple_of(((((n >> 1) ^ row) << 1) + (n & 1)) * size, size)


def attention_forward(place, q_ref, *refs, size, blocks):
    own_refs, other_refs, out_refs = refs[:4], refs[4:8], refs[8:12]
    inverse_ref, key_ref, value_ref, other_key_ref, other_value_ref = refs[12:]
    row, col, boundary = place[0], place[1], place[2]
    fill_keys(own_refs, key_ref, value_ref, None, row, col, boundary, size)
    fill_keys(other_refs, other_key_ref, other_value_ref, None, row, 1 - col, boundary, size)
    later = lax.broadcasted_iota(jnp.int32, (2 * size, size), 0) % size
    allowed = lax.broadcasted_iota(jnp.int32, (2 * size, size), 1) <= later
    lane = lane_of(size)

    def one_block(k, n, carry):
        i = 2 * k + n
        rows = pl.ds(pl.multiple_of(i * size, size), size)
        block = natural_block(i, row, col)
        queries = q_ref[rows, :]
        packed = [query_pieces(queries, block, size, boundary, g) for g in range(2)]

        def term(keys_from, values_from, start, g, diagonal):
            keys = pl.ds(start, size)
            weights = jnp.exp(dot_nt(packed[g], keys_from[g, keys, :]))
            if diagonal:
                weights = jnp.where(allowed, weights, 0.0)
            return dot(weights.astype(BF16), values_from[g, keys, :])

        def step(keys_from, values_from, m, sums):
            start = storage_of(m, row, size)
            return tuple(
                sums[g] + term(keys_from, values_from, start, g, False) for g in range(2)
            )

        first = jnp.where(block * size >= boundary, boundary // size, 0)
        start = pl.multiple_of(i * size, size)
        sums = tuple(term(key_ref, value_ref, start, g, True) for g in range(2))
        for part, sources in enumerate(((key_ref, value_ref), (other_key_ref, other_value_ref))):
            begin, end = own_before(first, col ^ part), own_before(block, col ^ part)
            sums = lax.fori_loop(begin, end, functools.partial(step, *sources), sums)
        for g in range(2):
            inverse = 1.0 / sums[g][:, 64:65]
            scaled = sums[g] * inverse
            columns = slice(g * LANES, (g + 1) * LANES)
            joined = jnp.where(lane < 64, scaled[:size], pltpu.roll(scaled[size:], 64, 1))
            out_refs[k][pl.ds(pl.multiple_of(n * size, size), size), columns] = joined.astype(BF16)
            inverse_ref[rows, columns] = jnp.where(lane < 64, inverse[:size], inverse[size:])
        return carry

    for k in range(4):
        lax.fori_loop(0, 2, functools.partial(one_block, k), 0)


def attention_backward(place, q_ref, *refs, size, blocks, part):
    kv_refs, out_refs, inverse_ref, grad_refs = refs[:4], refs[4:8], refs[8], refs[9:13]
    if part == 1:
        dkv_ref, dq_sum = refs[13:15]
    else:
        earlier_ref, dkv_ref, dq_ref, dq_sum = refs[13:17]
    key_ref, value_ref, turned_ref, packed_ref, packed_grad_ref, dk_sum, dv_sum = refs[-7:]
    row, col, boundary = place[0], place[1], place[2]
    lane = lane_of(size)
    fill_keys(kv_refs, key_ref, value_ref, turned_ref, row, col ^ part, boundary, size)

    def fill(k, n, carry):
        i = 2 * k + n
        rows = pl.ds(pl.multiple_of(i * size, size), size)
        inner = pl.ds(pl.multiple_of(n * size, size), size)
        block = natural_block(i, row, col)
        wide = pl.ds(pl.multiple_of(i * 2 * size, 2 * size), 2 * size)
        queries = q_ref[rows, :]
        for g in range(2):
            columns = slice(g * LANES, (g + 1) * LANES)
            packed_ref[g, wide, :] = query_pieces(queries, block, size, boundary, g)
            scaled = grad_refs[k][inner, columns].astype(F32) * inverse_ref[rows, columns]
            product = scaled * out_refs[k][inner, columns].astype(F32)
            pieces = []
            for w in (0, 1):
                total = -jnp.sum(
                    jnp.where((lane >= 64) if w else (lane < 64), product, 0.0), axis=1, keepdims=True
                )
                high = total.astype(BF16).astype(F32)
                extra = jnp.where(lane == 64, high, jnp.where(lane == 65, total - high, 0.0))
                pieces.append(jnp.where(lane < 64, half_pick(scaled, w), extra).astype(BF16))
            packed_grad_ref[g, wide, :] = jnp.concatenate(pieces, axis=0)
            if part == 1:
                dq_sum[g, :, wide] = jnp.zeros((64, 2 * size), F32)
            else:
                dq_sum[g, :, wide] = earlier_ref[g, :, wide]
        return carry

    for k in range(4):
        lax.fori_loop(0, 2, functools.partial(fill, k), 0)
    later = lax.broadcasted_iota(jnp.int32, (size, 2 * size), 1) % size
    allowed = lax.broadcasted_iota(jnp.int32, (size, 2 * size), 0) <= later

    def pair(start, i, diagonal):
        keys = pl.ds(start, size)
        wide = pl.ds(pl.multiple_of(i * 2 * size, 2 * size), 2 * size)
        for g in range(2):
            queries = packed_ref[g, wide, :]
            grads = packed_grad_ref[g, wide, :]
            weights = jnp.exp(dot_nt(key_ref[g, keys, :], queries))
            if diagonal:
                weights = jnp.where(allowed, weights, 0.0)
            change = dot_nt(value_ref[g, keys, :], grads)
            score = (weights * change).astype(BF16)
            value_term = dot(weights.astype(BF16), grads)
            key_term = dot(score, queries)
            if diagonal:
                dv_sum[g] = value_term
                dk_sum[g] = key_term
            else:
                dv_sum[g] += value_term
                dk_sum[g] += key_term
            dq_sum[g, :, wide] += dot(turned_ref[64 * g : 64 * (g + 1), keys], score)

    def one_block(i, carry):
        block = natural_block(i, row, col ^ part)
        start = pl.multiple_of(i * size, size)
        last = jnp.where((block + 1) * size <= boundary, (boundary - 1) // size, 2 * blocks - 1)
        begin = own_before(block, col) + 1 - part
        end = own_before(last + 1, col)
        if part == 0:
            pair(start, i, True)
        else:
            dk_sum[...] = jnp.zeros_like(dk_sum)
            dv_sum[...] = jnp.zeros_like(dv_sum)

        def step(n, carry):
            pair(start, (((n >> 1) ^ row) << 1) + (n & 1), False)
            return carry

        lax.fori_loop(begin, end, step, 0)
        rows = pl.ds(start, size)
        kind = dkv_ref.dtype
        key_grad = jnp.where(lane < 64, dk_sum[0], pltpu.roll(dk_sum[1], 64, 1))
        value_grad = jnp.where(lane < 64, dv_sum[0], pltpu.roll(dv_sum[1], 64, 1))
        dkv_ref[rows, :LANES] = key_grad.astype(kind)
        dkv_ref[rows, LANES:] = value_grad.astype(kind)
        return carry

    lax.fori_loop(0, blocks, one_block, 0)
    if part == 1:
        return

    def finish(i, carry):
        rows = pl.ds(pl.multiple_of(i * size, size), size)
        for g in range(2):
            wide = pl.multiple_of(i * 2 * size, 2 * size)
            stacked = jnp.concatenate(
                [dq_sum[g, :, pl.ds(wide, size)], dq_sum[g, :, pl.ds(wide + size, size)]], axis=0
            )
            dq_ref[rows, g * LANES : (g + 1) * LANES] = stacked.T
        return carry

    lax.fori_loop(0, blocks, finish, 0)


def head_totals(values):
    a = lax.broadcasted_iota(jnp.int32, (LANES, LANES), 0) // 64
    b = lax.broadcasted_iota(jnp.int32, (LANES, LANES), 1) // 64
    same = jnp.where(a == b, 1.0, 0.0).astype(BF16)
    high = values.astype(BF16)
    low = (values - high.astype(F32)).astype(BF16)
    return dot(high, same) + dot(low, same)


def turned_lanes(values):
    first = lane_of(values.shape[0]) % 64 < 32
    return jnp.where(first, pltpu.roll(values, LANES - 32, 1), pltpu.roll(values, 32, 1))


def prepare_kernel(
    left_ref, right_ref, w_mine, w_got, cos_ref, sin_ref, gain_ref, wide_gain_ref, *refs, scale, width
):
    q_ref, kv_ref, pre_ref, normed_ref = refs[-4:]
    left, right = left_ref[...].astype(F32), right_ref[...].astype(F32)
    squares = jnp.sum(left * left, axis=1, keepdims=True) + jnp.sum(
        right * right, axis=1, keepdims=True
    )
    inverse = lax.rsqrt(squares / (2 * width) + EPSILON)
    left = (left * inverse * wide_gain_ref[:, :width]).astype(BF16)
    right = (right * inverse * wide_gain_ref[:, width:]).astype(BF16)
    normed_ref[:, :width] = left
    normed_ref[:, width:] = right
    pre = dot(left, w_mine[...]) + dot(right, w_got[...])
    pre_ref[...] = pre[:, : 3 * LANES]
    for n in range(3):
        values = pre[:, n * LANES : (n + 1) * LANES]
        inverse = lax.rsqrt(head_totals(values * values) / 64 + EPSILON)
        normed = values * inverse * gain_ref[(0 if n < 2 else 1) : (1 if n < 2 else 2), :]
        rotated = normed * cos_ref[...] + turned_lanes(normed) * sin_ref[...]
        if n < 2:
            q_ref[:, n * LANES : (n + 1) * LANES] = (
                rotated.astype(BF16).astype(F32) * scale
            ).astype(BF16)
        else:
            kv_ref[:, :LANES] = rotated.astype(BF16)
    kv_ref[:, LANES:] = pre[:, 3 * LANES :].astype(BF16)


def prepare_back_kernel(
    pre_ref,
    cos_ref,
    sin_ref,
    gain_ref,
    dq_ref,
    own_ref,
    got_ref,
    w_mine,
    w_got,
    normed_ref,
    *refs,
    scale,
    width,
):
    out_ref, sums_ref, gain_sums_ref, grad_out_ref = refs[-4:]

    @pl.when(pl.program_id(0) == 0)
    def _():
        sums_ref[...] = jnp.zeros_like(sums_ref)
        gain_sums_ref[...] = jnp.zeros_like(gain_sums_ref)

    pieces = []
    for n in range(3):
        columns = slice(n * LANES, (n + 1) * LANES)
        values = pre_ref[:, columns]
        inverse = lax.rsqrt(head_totals(values * values) / 64 + EPSILON)
        if n < 2:
            grad = dq_ref[:, columns] * scale
        else:
            grad = own_ref[:, :LANES] + got_ref[:, :LANES].astype(F32)
        grad = grad * cos_ref[...] - turned_lanes(grad) * sin_ref[...]
        hat = values * inverse
        sums_ref[0:1, columns] += jnp.sum(grad * hat, axis=0, keepdims=True)
        scaled = grad * gain_ref[(0 if n < 2 else 1) : (1 if n < 2 else 2), :]
        mean = head_totals(scaled * hat) / 64
        pieces.append((inverse * (scaled - hat * mean)).astype(BF16))
    pieces.append((own_ref[:, LANES:] + got_ref[:, LANES:].astype(F32)).astype(BF16))
    grads = jnp.concatenate(pieces, axis=1)
    out_ref[...] = grads
    for half, w_ref in enumerate((w_mine, w_got)):
        columns = slice(half * width, (half + 1) * width)
        term = dot_nt(grads, w_ref[...])
        grad_out_ref[:, columns] = term.astype(BF16)
        product = term * normed_ref[:, columns].astype(F32)
        gain_sums_ref[0:1, columns] += jnp.sum(product, axis=0, keepdims=True)


def feed_forward_kernel(
    x_one, x_two, left_one, left_two, right_one, right_two,
    gate_mine, gate_got, up_mine, up_got, down_mine, down_got, *refs, width,
):
    hidden_ref, gate_grad_ref, up_grad_ref, x_out_ref, cot_out_ref = refs[-8:-3]
    back_one, back_two, total = refs[-3:]
    step = hidden_ref.shape[1]
    x = jnp.concatenate([x_one[...], x_two[...]], axis=0)
    left = jnp.concatenate([left_one[...], left_two[...]], axis=0)
    right = jnp.concatenate([right_one[...], right_two[...]], axis=0)

    @pl.when(pl.program_id(0) == 0)
    def _():
        x_out_ref[...] = x
        cot_out_ref[:, :width] = left
        cot_out_ref[:, width:] = right

    mine = jnp.concatenate([gate_mine[...], up_mine[...]], axis=1)
    got = jnp.concatenate([gate_got[...], up_got[...]], axis=1)
    both = dot(x[:, :width], mine) + dot(x[:, width:], got)
    gate, up = both[:, :step], both[:, step:]
    grad = dot_nt(left, down_mine[...]) + dot_nt(right, down_got[...])
    sigmoid = 1.0 / (1.0 + jnp.exp(-gate))
    silu = gate * sigmoid
    hidden_ref[...] = (silu * up).astype(BF16)
    gate_grad = (grad * up * (sigmoid + silu * (1.0 - sigmoid))).astype(BF16)
    up_grad = (grad * silu).astype(BF16)
    gate_grad_ref[...] = gate_grad
    up_grad_ref[...] = up_grad
    grads = jnp.concatenate([gate_grad, up_grad], axis=1)
    one, two = dot_nt(grads, mine), dot_nt(grads, got)

    @pl.when(pl.program_id(0) == 0)
    def _():
        total[:, :width] = one
        total[:, width:] = two

    @pl.when(pl.program_id(0) > 0)
    def _():
        total[:, :width] += one
        total[:, width:] += two

    @pl.when(pl.program_id(0) == pl.num_programs(0) - 1)
    def _():
        rows = back_one.shape[0]
        back_one[...] = total[:rows, :].astype(BF16)
        back_two[...] = total[rows:, :].astype(BF16)


def norm_rows(values, gain):
    inverse = lax.rsqrt(jnp.mean(values * values, axis=1, keepdims=True) + EPSILON)
    return (values * inverse * gain).astype(BF16), inverse


def norm_backward(values, inverse, gain, grad):
    gain_grad = jnp.sum(grad * values * inverse, axis=0)
    scaled = grad * gain
    inner = jnp.mean(scaled * values, axis=1, keepdims=True)
    return scaled * inverse - values * (inverse * inverse * inverse * inner), gain_grad


def body(
    tokens,
    seq_lengths,
    attn_gain,
    q_weight,
    k_weight,
    v_weight,
    q_gain,
    k_gain,
    o_weight,
    ffn_gain,
    gate_weight,
    up_weight,
    down_weight,
    cotangent,
):
    row, col = lax.axis_index("row"), lax.axis_index("col")
    local_rows, width = tokens.shape
    size = local_rows // 4
    own_rows = 2 * size
    blocks = 8
    all_rows = blocks * size
    head = q_gain.shape[0]
    scale = head ** (-0.5)
    hidden_cols = gate_weight.shape[1]
    boundary = seq_lengths[0, 0]

    def mine(x):
        outer = jnp.concatenate([x[:size], x[3 * size :]], axis=0)
        inner = x[size : 3 * size]
        return jnp.where(col == 0, outer, inner), jnp.where(col == 0, inner, outer)

    def to_whole(x):
        keep, give = mine(x)
        return jnp.concatenate([keep, swap(give, "col", 1)], axis=1)

    def from_whole(keep, got):
        outer = jnp.where(col == 0, keep, got)
        inner = jnp.where(col == 0, got, keep)
        return jnp.concatenate([outer[:size], inner, outer[size:]], axis=0)

    def both(x, axis):
        return jnp.concatenate([x, swap(x, "col", 1)], axis=axis)

    def through_dp(x, anchor):
        part = x.shape[0] // lax.axis_size("dp")
        piece = lax.dynamic_slice_in_dim(x, lax.axis_index("dp") * part, part)
        return swap(after(piece, anchor), "col", 1)

    keep, give = mine(tokens)
    got = swap(give, "col", 1)
    w_mine = jnp.concatenate([q_weight, k_weight, v_weight], axis=1)
    w_got = swap(after(w_mine, got), "col", 1)
    gains = both(jnp.stack([attn_gain, ffn_gain]), 1)

    index = jnp.arange(all_rows, dtype=jnp.int32)
    token = natural_block(index // size, row, col) * size + index % size
    position = jnp.where(token >= boundary, token - boundary, token)
    lane = jnp.arange(LANES, dtype=jnp.int32)
    frequency = ROPE_BASE ** (-((jnp.arange(head // 2, dtype=F32)) * 2.0) / head)
    angle = position.astype(F32)[:, None] * frequency[None, :]
    cos_table = jnp.tile(jnp.cos(angle), (1, LANES // (head // 2)))
    sin_table = jnp.tile(jnp.sin(angle), (1, LANES // (head // 2)))
    sin_table = jnp.where((lane % head < head // 2)[None, :], -sin_table, sin_table)
    head_gains = jnp.stack([jnp.tile(q_gain, 2), jnp.tile(k_gain, 2)])

    got, cos_table, sin_table, gains = lax.optimization_barrier(
        (got, cos_table, sin_table, gains)
    )
    gain_one, gain_two = gains[0], gains[1]
    left, right = gather_row(keep), gather_row(got)
    inputs = jnp.concatenate([keep, got], axis=1).astype(F32)
    inverse_one = lax.rsqrt(jnp.mean(inputs * inputs, axis=1, keepdims=True) + EPSILON)

    def tile(columns, first=0):
        return pl.BlockSpec((size, columns), lambda i: (i + first, 0))

    def fixed(x):
        return pl.BlockSpec(x.shape, lambda i: (0, 0))

    def rows_of(count, columns, kind):
        return jax.ShapeDtypeStruct((count, columns), kind)

    anywhere = pl.BlockSpec(memory_space=pl.ANY)
    params = pltpu.CompilerParams(vmem_limit_bytes=VMEM_LIMIT)
    wide_gain = gain_one[None, :]

    def prepare(k, earlier):
        return pl.pallas_call(
            functools.partial(prepare_kernel, scale=scale, width=width),
            grid=(2,),
            in_specs=[tile(width), tile(width), fixed(w_mine), fixed(w_got)]
            + [tile(LANES, 2 * k)] * 2
            + [fixed(head_gains), fixed(wide_gain)]
            + [anywhere] * len(earlier),
            out_specs=[tile(256, 2 * k), tile(256), tile(384, 2 * k), tile(2 * width, 2 * k)],
            out_shape=[
                rows_of(all_rows, 256, BF16),
                rows_of(own_rows, 256, BF16),
                rows_of(all_rows, 384, F32),
                rows_of(all_rows, 2 * width, BF16),
            ],
            input_output_aliases={8 + n: m for n, m in enumerate((0, 2, 3)[: len(earlier)])},
            compiler_params=params,
            name="prepare",
        )(
            left[k], right[k], w_mine, w_got, cos_table, sin_table, head_gains, wide_gain, *earlier
        )

    kept, kv_own, kv_other = (), [], []
    for k in range(4):
        if k == 1:
            o_other = swap(after(o_weight, w_got), "col", 1)
            down_piece = through_dp(down_weight, w_got)
            left[1], o_other, down_piece = lax.optimization_barrier((left[1], o_other, down_piece))
            down_got = lax.all_gather(down_piece, "dp", axis=0, tiled=True)
            cot_keep, cot_give = mine(cotangent)
            cot_left = gather_row(after(cot_keep, kv_own[0]))
        if k == 3:
            left[3], kv_other[0], kv_other[1], cot_left[2] = lax.optimization_barrier(
                (left[3], kv_other[0], kv_other[1], cot_left[2])
            )
        queries, kv, pre, normed_one_all = prepare(k, kept)
        kept = (queries, pre, normed_one_all)
        kv_own.append(kv)
        kv_other.append(swap(kv, "col", 1))


    place = jnp.stack([row.astype(jnp.int32), col.astype(jnp.int32), boundary.astype(jnp.int32)])
    whole = pl.BlockSpec(memory_space=pltpu.VMEM)
    smem = pl.BlockSpec(memory_space=pltpu.SMEM)
    key_scratch = [pltpu.VMEM((2, all_rows, LANES), BF16)] * 2
    gate_up_give = jnp.concatenate([gate_weight, up_weight], axis=1)
    gate_up_got = swap(after(gate_up_give, kv_other[2], kv_other[3]), "col", 1)
    cot_got = swap(after(cot_give, kv_other[2], kv_other[3]), "col", 1)
    *attended, inverse_total = pl.pallas_call(
        functools.partial(attention_forward, size=size, blocks=blocks),
        in_specs=[smem] + [whole] * 9,
        out_specs=[whole] * 5,
        out_shape=[rows_of(own_rows, 256, BF16)] * 4 + [rows_of(all_rows, 256, F32)],
        scratch_shapes=key_scratch * 2,
        compiler_params=params,
        name="attend",
    )(place, queries, *kv_own, *kv_other)

    attended[0], down_got = lax.optimization_barrier((attended[0], down_got))
    w_o = jnp.concatenate(gather_row(jnp.concatenate([o_weight, o_other], axis=1)), axis=0)
    attended_own = jnp.concatenate(exchange_row(attended), axis=1)
    attended_own, gate_up_got = lax.optimization_barrier((attended_own, gate_up_got))
    residual = inputs + dot(attended_own, w_o)
    normed_two, inverse_two = norm_rows(residual, gain_two)
    cot_own = jnp.concatenate([cot_keep, cot_got], axis=1)
    cot_right = [cot_got, swap(cot_got, "row", 1), swap(after(cot_got, attended_own), "row", 2)]
    gathered = [normed_two, swap(normed_two, "row", 1), swap(normed_two, "row", 2)]
    hidden_cols = gate_weight.shape[1]
    ffn_weights = (gate_weight, gate_up_got, up_weight, gate_up_got, down_weight, down_got)
    hidden_step = hidden_cols // 3

    def feed_forward(pair, earlier):
        def part(rows, columns, fixed_row=0):
            return pl.BlockSpec((rows, columns), lambda i: (fixed_row, i))

        def still(rows, columns, fixed_row=0):
            return pl.BlockSpec((rows, columns), lambda i: (fixed_row, 0))

        down_spec = pl.BlockSpec((hidden_step, width), lambda i: (i, 0))
        ks = (2 * pair, 2 * pair + 1)
        return pl.pallas_call(
            functools.partial(feed_forward_kernel, width=width),
            grid=(3,),
            in_specs=[still(own_rows, 2 * width)] * 2
            + [still(own_rows, width)] * 4
            + [part(width, hidden_step)] * 3
            + [pl.BlockSpec((width, hidden_step), lambda i: (0, i + 3))]
            + [down_spec] * 2
            + [anywhere] * len(earlier),
            out_specs=[part(2 * own_rows, hidden_step, pair)] * 3
            + [still(2 * own_rows, 2 * width, pair)] * 2
            + [still(own_rows, 2 * width)] * 2,
            out_shape=[rows_of(all_rows, hidden_cols, BF16)] * 3
            + [rows_of(all_rows, 2 * width, BF16)] * 2
            + [rows_of(own_rows, 2 * width, BF16)] * 2,
            scratch_shapes=[pltpu.VMEM((2 * own_rows, 2 * width), F32)],
            input_output_aliases={12 + n: n for n in range(len(earlier))},
            compiler_params=params,
            name="feed_forward",
        )(
            *[gathered[k] for k in ks],
            *[cot_left[k] for k in ks],
            *[cot_right[k] for k in ks],
            *ffn_weights,
            *earlier,
        )

    *kept, back_0, back_1 = feed_forward(0, ())
    gathered.append(swap(after(gathered[2], back_0), "row", 1))
    cot_right.append(swap(after(cot_right[2], back_0), "row", 1))
    *kept, back_2, back_3 = feed_forward(1, kept)
    hidden, gate_grad, up_grad, normed_two_all, cot_all = kept
    backs = [back_0, back_1, back_2, back_3]
    back_far = far_sum(backs)
    normed_two_grad = scatter_row(backs, back_far)

    hidden_late, normed_late = after(hidden, back_far), after(normed_two_all, back_far)
    down_give = dot_tn(hidden, cot_all[:, width:]).astype(BF16)
    gate_give = dot_tn(normed_late[:, width:], gate_grad).astype(BF16)
    up_give = dot_tn(normed_late[:, width:], up_grad).astype(BF16)
    ffn_out = [
        jnp.concatenate([dot(part, down_weight), dot(part, down_got)], axis=1).astype(BF16)
        for part in [hidden_late[k * own_rows : (k + 1) * own_rows] for k in range(4)]
    ]
    down_other, gate_other, up_other = [swap(x, "col", 1) for x in (down_give, gate_give, up_give)]
    normed_two_grad, *ffn_out = lax.optimization_barrier((normed_two_grad, *ffn_out))
    residual_part, ffn_gain_grad = norm_backward(residual, inverse_two, gain_two, normed_two_grad)
    residual_grad = cot_own.astype(F32) + residual_part
    branch_grad = residual_grad.astype(BF16)
    attended_grad = dot_nt(branch_grad, w_o).astype(BF16)
    attended_grad = exchange_row([attended_grad[:, k * 256 : (k + 1) * 256] for k in range(4)])

    def add_other(keep, other):
        return (keep + other.astype(F32)).astype(BF16)

    down_grad = add_other(dot_tn(hidden, cot_all[:, :width]), down_other)
    gate_keep = dot_tn(normed_late[:, :width], gate_grad)
    up_keep = dot_tn(normed_late[:, :width], up_grad)
    down_grad = lax.psum_scatter(down_grad, "dp", scatter_dimension=0, tiled=True)
    down_grad, gate_keep, up_keep, *attended_grad = lax.optimization_barrier(
        (down_grad, gate_keep, up_keep, *attended_grad)
    )
    down_grad = lax.all_gather(down_grad, "dp", axis=0, tiled=True)

    ffn_out = scatter_row(ffn_out, after(far_sum(ffn_out), attended_grad[3]))
    output = (residual + ffn_out).astype(BF16)
    output = from_whole(output[:, :width], swap(output[:, width:], "col", 1))

    o_give = dot_tn(attended_own, branch_grad[:, width:]).astype(BF16)
    o_other = swap(o_give, "col", 1)
    o_rows = o_weight.shape[0]
    def attend_back(part, kv_parts, earlier):
        dq_shape = jax.ShapeDtypeStruct((2, 64, 2 * all_rows), F32)
        if part == 1:
            shapes, extra = [rows_of(all_rows, 256, BF16), dq_shape], []
        else:
            shapes = [rows_of(all_rows, 256, F32), rows_of(all_rows, 256, F32)]
            extra = [pltpu.VMEM(dq_shape.shape, F32)]
        return pl.pallas_call(
            functools.partial(attention_backward, size=size, blocks=blocks, part=part),
            in_specs=[smem] + [whole] * (14 + len(earlier)),
            out_specs=[whole] * 2,
            out_shape=shapes,
            scratch_shapes=extra
            + key_scratch
            + [
                pltpu.VMEM((LANES, all_rows), BF16),
                pltpu.VMEM((2, 2 * all_rows, LANES), BF16),
                pltpu.VMEM((2, 2 * all_rows, LANES), BF16),
                pltpu.VMEM((2, size, LANES), F32),
                pltpu.VMEM((2, size, LANES), F32),
            ],
            compiler_params=params,
            name="attend_back",
        )(place, queries, *kv_parts, *attended, inverse_total, *attended_grad, *earlier)

    dkv_other, dq_part = attend_back(1, kv_other, ())
    dkv_got = swap(dkv_other, "col", 1)
    gate_weight_grad = add_other(gate_keep, after(gate_other, dq_part))
    up_weight_grad = add_other(up_keep, after(up_other, dq_part))
    gate_up_grad = jnp.concatenate([gate_weight_grad, up_weight_grad], axis=1)
    dq_part, gate_up_grad, down_grad = lax.optimization_barrier((dq_part, gate_up_grad, down_grad))
    gate_up_grad = lax.psum_scatter(gate_up_grad, "dp", scatter_dimension=0, tiled=True)
    dkv_own, dq = attend_back(0, kv_own, (dq_part,))
    o_grad = add_other(dot_tn(attended_own, branch_grad[:, :width]), after(o_other, dq))
    o_grad = [o_grad[k * o_rows : (k + 1) * o_rows] for k in range(4)]
    o_grad = scatter_row(o_grad, far_sum(o_grad)).astype(BF16)

    def prepare_back(k, earlier):
        return pl.pallas_call(
            functools.partial(prepare_back_kernel, scale=scale, width=width),
            grid=(2,),
            in_specs=[tile(384, 2 * k), tile(LANES, 2 * k), tile(LANES, 2 * k), fixed(head_gains)]
            + [tile(256, 2 * k)] * 3
            + [fixed(w_mine), fixed(w_got), tile(2 * width, 2 * k)]
            + [anywhere] * len(earlier),
            out_specs=[
                tile(512, 2 * k),
                pl.BlockSpec((8, 3 * LANES), lambda i: (0, 0)),
                pl.BlockSpec((8, 2 * width), lambda i: (0, 0)),
                tile(2 * width),
            ],
            out_shape=[
                rows_of(all_rows, 512, BF16),
                rows_of(8, 3 * LANES, F32),
                rows_of(8, 2 * width, F32),
                rows_of(own_rows, 2 * width, BF16),
            ],
            input_output_aliases={10: 0} if earlier else {},
            compiler_params=params,
            name="prepare_back",
        )(
            pre, cos_table, sin_table, head_gains, dq, dkv_own, dkv_got, w_mine, w_got,
            normed_one_all, *earlier
        )

    kept, head_sums, gain_sums, backs = (), 0.0, 0.0, [None] * 4
    for k in (3, 2, 1, 0):
        projected_grad, one, two, backs[k] = prepare_back(k, kept)
        head_sums, gain_sums = head_sums + one, gain_sums + two
        if k == 2:
            back_far = far_sum(backs)
            projected_grad, back_far = lax.optimization_barrier((projected_grad, back_far))
        if k == 1:
            projected_grad, gate_up_grad = lax.optimization_barrier((projected_grad, gate_up_grad))
            gate_up_grad = lax.all_gather(gate_up_grad, "dp", axis=0, tiled=True)
        kept = (projected_grad,)
    normed_one_grad = scatter_row(backs, back_far)
    normed_one_grad, normed_one_all, gate_up_grad, output = lax.optimization_barrier(
        (normed_one_grad, normed_one_all, gate_up_grad, output)
    )
    attn_gain_grad = gain_sums[0] / gain_one
    qkv_other = swap(dot_tn(normed_one_all[:, width:], projected_grad).astype(BF16), "col", 1)
    qkv_grad = add_other(dot_tn(normed_one_all[:, :width], projected_grad), qkv_other)
    qkv_rows = qkv_grad.shape[0]
    joined = sum_dp(jnp.concatenate([qkv_grad, o_grad], axis=0))
    qkv_grad, o_grad = joined[:qkv_rows], joined[qkv_rows:]
    input_part, _ = norm_backward(inputs, inverse_one, gain_one, normed_one_grad)
    input_grad = residual_grad + input_part
    input_grad = from_whole(
        input_grad[:, :width], swap(after(input_grad[:, width:].astype(BF16), qkv_other), "col", 1).astype(F32)
    )

    head_sums = head_sums[0].reshape(6, head)
    q_sum, k_sum = jnp.sum(head_sums[:4], axis=0), jnp.sum(head_sums[4:], axis=0)
    small = jnp.concatenate([attn_gain_grad[:width], ffn_gain_grad[:width], q_sum, k_sum])
    given = jnp.concatenate([attn_gain_grad[width:], ffn_gain_grad[width:], q_sum, k_sum])
    small, given = after(small, normed_one_grad), after(given, normed_one_grad)
    small = small + swap(given, "col", 1)
    for axis in ("row", "dp"):
        distance = 1
        while distance < lax.axis_size(axis):
            small = small + swap(small, axis, distance)
            distance *= 2
    attn_gain_grad, ffn_gain_grad = small[:width], small[width : 2 * width]
    q_gain_grad, k_gain_grad = small[2 * width : 2 * width + head], small[2 * width + head :]
    query_cols, kv_cols = q_weight.shape[1], k_weight.shape[1]
    qkv_grad = qkv_grad.astype(F32)
    return (
        output,
        input_grad,
        attn_gain_grad,
        qkv_grad[:, :query_cols],
        qkv_grad[:, query_cols : query_cols + kv_cols],
        qkv_grad[:, query_cols + kv_cols :],
        q_gain_grad,
        k_gain_grad,
        o_grad.astype(F32),
        ffn_gain_grad,
        gate_up_grad[:, :hidden_cols].astype(F32),
        gate_up_grad[:, hidden_cols:].astype(F32),
        down_grad.astype(F32),
    )


def solution(mesh):
    in_specs = (
        P(("dp", "row"), "col"),
        P("dp", None),
        P("col"),
        P("col", "row"),
        P("col", "row"),
        P("col", "row"),
        P(),
        P(),
        P("row", "col"),
        P("col"),
        P("col", "row"),
        P("col", "row"),
        P("row", "col"),
        P(("dp", "row"), "col"),
    )
    out_specs = (
        P(("dp", "row"), "col"),
        P(("dp", "row"), "col"),
        P("col"),
        P("col", "row"),
        P("col", "row"),
        P("col", "row"),
        P(),
        P(),
        P("row", "col"),
        P("col"),
        P("col", "row"),
        P("col", "row"),
        P("row", "col"),
    )
    return jax.shard_map(body, mesh=mesh, in_specs=in_specs, out_specs=out_specs, check_vma=False)
```
